512 devices in a mesh: row: 32 (over z, x_lo, core), rep: 16 (over x_hi, y).
Axes of the slice: x: 4 (x_hi: 2, x_lo: 2; x = x_hi * 2 + x_lo), y: 8, z: 8, core: 2. Of those that a mesh axis runs over, the one named last changes fastest.
Arguments:
- feats: bfloat16 [32768, 256], P('row'), may hold values from -6 to 6
- weight: bfloat16 [256, 256], replicated, may hold values from -0.375 to 0.375
- weight_mask: int32 [256, 256], replicated, may hold values 0 or 1
- tile_vals: bfloat16 [6144, 128, 128], P(('row', 'rep')), may hold values from -0.109375 to 0.109375
- edge_mask: float32 [6144, 128, 128], P(('row', 'rep')), may hold values from 0.25 to 2
- tile_pos: int32 [6144], P(('row', 'rep')), may hold values from -1 to 127, as said below
- grad_out: bfloat16 [32768, 256], P('row'), may hold values from -6 to 6
Outputs:
- out_feats: bfloat16 [32768, 256], P('row')
- feature_gradient: bfloat16 [32768, 256], P('row')
- weight_gradient: float32 [256, 256], replicated
- grad_edge: float32 [6144, 128, 128], P(('row', 'rep'))
The draws below stay inside these ranges and needn't reach their ends.
Inputs may be any that keep to these rules, and one draw needn't show every extreme that they name: `tile_pos`: entries of one device (d * 12 onward) hold distinct tile positions below 128 first and -1 after them; at least one entry of every device is live, and some device has all 12 live.
All inputs are finite; a program needn't handle non-finite values.
Results may differ from the reference program's by a relative error of at most 0.0058.
Values may be sent and summed in bfloat16 or wider, within the bound.
A program may use at most 64 MiB of HBM per device.

```python
import jax
import jax.numpy as jnp
from jax import lax

F = 256
TILE = 128
NODES_BLK = 1024
TILES_DEV = 12
TB = 8
SLOTS = 128
MESH_DEVICES = 512
NODES = 32768
TILE_ENTRY_COUNT = 6144
N_REP = 16


def draw_tile_pos(key, part):
    key = jax.random.fold_in(key, 11)
    perm_key, count_key, full_key = jax.random.split(key, 3)
    dev_keys = jax.random.split(perm_key, MESH_DEVICES)
    picks = jax.vmap(lambda one: jax.random.permutation(one, SLOTS)[:TILES_DEV])(dev_keys)
    divisor = 1 + jax.random.randint(count_key, (MESH_DEVICES,), 0, 4)
    counts = jnp.maximum(TILES_DEV // divisor, 1)
    fullest = jax.random.randint(full_key, (), 0, MESH_DEVICES)
    counts = jnp.where(jnp.arange(MESH_DEVICES) == fullest, TILES_DEV, counts)
    alive = jnp.arange(TILES_DEV)[None, :] < counts[:, None]
    return jnp.where(alive, picks, -1).reshape(-1).astype(jnp.int32)


def plant(result, key, smallest, high):
    longest = result.shape.index(max(result.shape))
    spots = []
    for shift in (0, 1):
        where = [jax.random.randint(jax.random.fold_in(key, axis), (), 0, length) for axis, length in enumerate(result.shape)]
        where[longest] = (where[longest] + shift) % result.shape[longest]
        spots.append(tuple(where))
    return result.at[spots[0]].set(smallest).at[spots[1]].set(high)


def steps_of(rng, shape, pieces, least, top_value):
    factor_of, own = 1.0, jax.random.fold_in(rng, 6)
    for axis_at, shards_of in pieces:
        heights = jnp.exp(jax.random.uniform(jax.random.fold_in(own, axis_at), (shards_of,), jnp.float32, least / len(pieces), top_value / len(pieces)))
        factor_of = factor_of * jnp.repeat(heights, shape[axis_at] // shards_of).reshape([-1 if axis == axis_at else 1 for axis in range(len(shape))])
    return factor_of


def scatter_about(key, shape, spread, reach, pieces=(), kind=jnp.bfloat16):
    gain = steps_of(key, shape, pieces, -0.22, 0.18) if pieces else 1.0
    result = jax.random.normal(key, shape, jnp.float32) * spread * gain
    return jnp.minimum(jnp.maximum(result, -reach), reach).astype(kind)


def setup_inputs(seed: int = 0) -> dict:
    streams_of = jax.random.split(jax.random.key(seed), 8)
    feats = scatter_about(streams_of[0], (NODES, F), 1.0, 6.0, ((0, 32),))
    weight = scatter_about(streams_of[1], (F, F), F ** -0.5, 0.375)
    weight_mask = plant((jax.random.randint(streams_of[2], (F, F), 0, 5) < 4).astype(jnp.int32), jax.random.fold_in(streams_of[2], 1), 0, 1)
    tile_vals = scatter_about(streams_of[3], (TILE_ENTRY_COUNT, TILE, TILE), (TILES_DEV * N_REP * TILE // TB) ** -0.5, 0.109375, ((0, 512),))
    edge_mask = jnp.clip(0.25 + 1.75 * jax.random.uniform(streams_of[4], (TILE_ENTRY_COUNT, TILE, TILE), jnp.float32) ** steps_of(streams_of[4], (TILE_ENTRY_COUNT, TILE, TILE), ((0, 512),), -0.2, 0.2), 0.25, 2.0)
    tile_pos = draw_tile_pos(jax.random.fold_in(streams_of[7], 71), 0)
    grad_out = scatter_about(streams_of[6], (NODES, F), 1.0, 6.0, ((0, 32),))
    return {"feats": feats, "weight": weight, "weight_mask": weight_mask, "tile_vals": tile_vals, "edge_mask": edge_mask, "tile_pos": tile_pos, "grad_out": grad_out}


def reference(feats, weight, weight_mask, tile_vals, edge_mask, tile_pos, grad_out):
    per_side = NODES_BLK // TILE
    w_eff = jnp.where(weight_mask != 0, weight, jnp.zeros_like(weight))
    proj = jnp.dot(feats, w_eff, preferred_element_type=jnp.float32).astype(jnp.bfloat16)
    masked = (tile_vals.astype(jnp.float32) * edge_mask).astype(jnp.bfloat16)
    device = jnp.arange(TILE_ENTRY_COUNT, dtype=jnp.int32) // TILES_DEV
    row_block = device // N_REP
    rep_index = device % N_REP
    live = tile_pos >= 0
    slot = jnp.maximum(tile_pos, 0)
    section = slot // (per_side * per_side)
    tile_row = (slot // per_side) % per_side
    tile_col = slot % per_side
    glob_row = (row_block * per_side + tile_row).astype(jnp.int32)
    glob_col = ((section * N_REP + rep_index) * per_side + tile_col).astype(jnp.int32)
    projected_tiles = proj.reshape(NODES // TILE, TILE, F)
    tile_gradients = grad_out.reshape(NODES // TILE, TILE, F)

    def shaped(values):
        return values.reshape((MESH_DEVICES, TILES_DEV) + values.shape[1:])

    def visit(carry, items):
        out_acc, column_running_sum = carry
        mask_tiles, raw_tiles, rows, cols, alive = items
        adj = mask_tiles.astype(jnp.float32)
        right = projected_tiles[cols].astype(jnp.float32)
        left = tile_gradients[rows].astype(jnp.float32)
        alive_f = alive.astype(jnp.float32)[:, None, None]
        out_acc = out_acc.at[rows].add(jnp.einsum("tab,tbf->taf", adj, right) * alive_f)
        column_running_sum = column_running_sum.at[cols].add(jnp.einsum("tab,taf->tbf", adj, left) * alive_f)
        edge_part = raw_tiles.astype(jnp.float32) * jnp.einsum("taf,tbf->tab", left, right) * alive_f
        return (out_acc, column_running_sum), edge_part

    start = jnp.zeros((NODES // TILE, TILE, F), jnp.float32)
    (out_acc, column_running_sum), edge_parts = lax.scan(
        visit, (start, start),
        (shaped(masked), shaped(tile_vals), shaped(glob_row), shaped(glob_col), shaped(live)))
    out_feats = out_acc.reshape(NODES, F).astype(jnp.bfloat16)
    grad_cols = column_running_sum.reshape(NODES, F).astype(jnp.bfloat16)
    feature_gradient = lax.dot_general(grad_cols, w_eff, (((1,), (1,)), ((), ())),
                                 preferred_element_type=jnp.float32).astype(jnp.bfloat16)
    full_weight = lax.dot_general(feats, grad_cols, (((0,), (0,)), ((), ())),
                                  preferred_element_type=jnp.float32)
    weight_gradient = jnp.where(weight_mask != 0, full_weight, jnp.zeros_like(full_weight))
    grad_edge = edge_parts.reshape(TILE_ENTRY_COUNT, TILE, TILE)
    return out_feats, feature_gradient, weight_gradient, grad_edge
```

```python
import functools

import jax
import jax.numpy as jnp
from jax import lax
from jax.experimental import pallas as pl
from jax.experimental.pallas import tpu as pltpu
from jax.sharding import PartitionSpec as P

BF = jnp.bfloat16
F32 = jnp.float32


def semaphore_places(n):
    counts = dict(
        a1=2, a2=n, a3=n, a4=2 * n,
        d1=2 * n, d2=n, d3=n, d4=2, d5=n, d6=n,
        c1=n, c2=n, c3=n, c4=n,
        wz=n, wc=4, wy=n, wx=n,
    )
    places, total = {}, 0
    for name, count in counts.items():
        places[name] = total
        total += count
    return places, total


def loop(low, high, step):
    def run(i, carry):
        step(i)
        return carry

    lax.fori_loop(low, high, run, 0)


def kernel(
    n, places,
    pos_ref, feats_h, gout_h, w_h, wm_h, tv_h, em_h,
    out_h, fg_h, wg_h, ge_h,
    feats, gout, w, wm, tv, em,
    weff, a1s, pj, mk, mkt, gs, rs, lhs, pb,
    d1r, d2s, d2r, d3s, d3r, d3o, d4s, gc,
    yb, c1r, c2s, c2r, c2o, oc,
    ft, wp, wz, wc, wa, wgo, ge, fg,
    send, recv, local,
):
    row, rep = lax.axis_index("row"), lax.axis_index("rep")
    z, xl, c = row // 4, row // 2 % 2, row % 2
    xh, y = rep // n, rep % n
    reps = 2 * n
    tiles, side, _ = tv.shape
    width = w.shape[0]
    piece_rows = pj.shape[2]
    per_side = gout.shape[0]
    ppt = side // piece_rows
    block = per_side * side

    def row_of(zz, xx, cc):
        return zz * 4 + xx * 2 + cc

    core_row, lo_row, both_row = row_of(z, xl, 1 - c), row_of(z, 1 - xl, c), row_of(z, 1 - xl, 1 - c)
    hi_rep = (1 - xh) * n + y
    mine = (c * 2 + xl) * n + z

    def around(at, o):
        return lax.rem(at + o, n)

    def copy(name, i, j, src, dst, to_row, to_rep):
        return pltpu.make_async_remote_copy(
            src_ref=src,
            dst_ref=dst,
            send_sem=send.at[places[name] + i],
            recv_sem=recv.at[places[name] + j],
            device_id=(to_row, to_rep),
            device_id_type=pl.DeviceIdType.MESH,
        )

    def arrived(name, j, ref):
        copy(name, 0, j, ref, ref, core_row, rep).wait_recv()

    def left(name, i, ref):
        copy(name, i, 0, ref, ref, core_row, rep).wait_send()

    owner_rows, owner_rep = [k * reps + rep for k in range(2)], mine // 2
    own_half = lax.rem(mine, 2)
    section, group = row // reps, lax.rem(row, reps)
    part_rows, parts = [], []
    for e in range(2):
        p = 2 * rep + e
        parts.append(p)
        part_rows.append(row_of(lax.rem(p, n), lax.rem(p // n, 2), p // (2 * n)))

    def is_me(r, q):
        return jnp.logical_and(r == row, q == rep)

    ins = []
    for i, (src, dst) in enumerate(
        ((w_h, w), (wm_h, wm), (feats_h, feats), (tv_h, tv), (em_h, em), (gout_h, gout))
    ):
        ins.append(pltpu.make_async_copy(src, dst, local.at[i]))
        ins[-1].start()

    barrier = pltpu.get_barrier_semaphore()

    def greet(r, q):
        pl.semaphore_signal(barrier, inc=1, device_id=(r, q), device_id_type=pl.DeviceIdType.MESH)

    greet(core_row, rep)
    greet(lo_row, rep)
    greet(both_row, rep)
    greet(row, hi_rep)
    loop(1, n, lambda o: greet(row_of(around(z, o), xl, c), rep))
    loop(1, n, lambda o: greet(row, xh * n + around(y, o)))
    expected = 4 + 2 * (n - 1)
    for k in range(2):
        for r, q in ((owner_rows[k], owner_rep), (part_rows[k], group)):
            other = jnp.logical_not(is_me(r, q))
            pl.when(other)(functools.partial(greet, r, q))
            expected = expected + other.astype(jnp.int32)

    ins[0].wait()
    ins[1].wait()
    weff[...] = jnp.where(wm[...] != 0, w[...].astype(F32), 0.0).astype(BF)
    ins[2].wait()
    piece = jnp.dot(feats[rep], weff[...], preferred_element_type=F32).astype(BF)
    a1s[...] = piece.reshape(a1s.shape)

    pl.semaphore_wait(barrier, expected)

    def scatter_piece(e):
        src, dst = a1s.at[e], pj.at[parts[e], section]
        same = is_me(part_rows[e], group)

        @pl.when(jnp.logical_not(same))
        def _():
            copy("a1", e, section, src, dst, part_rows[e], group).start()

        @pl.when(same)
        def _():
            pltpu.make_async_copy(src, dst, recv.at[places["a1"] + section]).start()

    scatter_piece(0)
    scatter_piece(1)

    picks = []
    for t in range(tiles):
        pos = pos_ref[t]
        slot = jnp.maximum(pos, 0)
        picks.append(
            (
                pos >= 0,
                lax.rem(slot // per_side, per_side),
                slot // (per_side * per_side),
                lax.rem(slot, per_side),
            )
        )

    ins[3].wait()
    ins[4].wait()
    ins[5].wait()
    for t in range(tiles):
        product = tv[t].astype(F32) * em[t]
        mk[t] = product.astype(BF)
        mkt[t] = product.T.astype(BF)
        gs[t] = gout[picks[t][1]]

    def chosen(cond, tile):
        return lax.select_n(cond, jnp.zeros_like(tile), tile)

    def backward_tile(jj):
        for k in range(2):
            for t in range(tiles):
                live, _, kt, jt = picks[t]
                cond = jnp.logical_and(live, jnp.logical_and(kt == k, jt == jj))
                lhs[k * side:(k + 1) * side, t * side:(t + 1) * side] = chosen(cond, mkt[t])
        total = jnp.dot(lhs[...], gs[...].reshape(tiles * side, width), preferred_element_type=F32)
        total = total.astype(BF)
        for k in range(2):
            pb[pl.ds(jj * ppt, ppt), k] = total[k * side:(k + 1) * side].reshape(ppt, piece_rows, width)

    quarter_tiles = n // ppt

    def send_quarter(x):
        def one(i):
            m = x * n + i
            copy("d1", m, m, pb.at[(1 - c) * 2 * n + m], d1r.at[m], core_row, rep).start()

        first = ((1 - c) * 2 + x) * quarter_tiles
        loop(0, quarter_tiles, lambda i: backward_tile(first + i))
        loop(0, n, one)

    send_quarter(1 - xl)
    send_quarter(xl)

    arrived("a1", 0, a1s.at[0])
    arrived("a1", 1, a1s.at[0])

    def pass_lo(zz):
        p = (c * 2 + xl) * n + zz
        copy("a3", zz, zz, pj.at[p], pj.at[p], lo_row, rep).start()

    def pass_core(m):
        p = c * 2 * n + m
        copy("a4", m, m, pj.at[p], pj.at[p], core_row, rep).start()

    def pass_z(o):
        zz = around(z, o)
        copy("a2", zz, z, pj.at[mine], pj.at[mine], row_of(zz, xl, c), rep).start()

    pass_lo(z)
    loop(1, n, pass_z)
    pass_core(xl * n + z)

    loop(0, 2 * quarter_tiles, lambda i: backward_tile(c * 2 * quarter_tiles + i))

    def d2_step(o):
        zz = around(z, o)
        m = (1 - xl) * n + zz
        arrived("d1", m, d1r.at[m])
        d2s[zz] = (pb[c * 2 * n + m].astype(F32) + d1r[m].astype(F32)).astype(BF)
        copy("d2", zz, zz, d2s.at[zz], d2r.at[zz], lo_row, rep).start()

    loop(1, n + 1, d2_step)

    def a2_step(o):
        zz = around(z, o)
        arrived("a2", zz, a2_like)
        pass_lo(zz)
        pass_core(xl * n + zz)

    a2_like = pj.at[mine]
    loop(1, n, a2_step)

    def d3_sum(zz):
        m = xl * n + zz
        arrived("d1", m, d1r.at[m])
        arrived("d2", zz, d2r.at[zz])
        return pb[c * 2 * n + m].astype(F32) + d1r[m].astype(F32) + d2r[zz].astype(F32)

    def d3_step(o):
        zz = around(z, o)
        d3s[zz] = d3_sum(zz).astype(BF)
        copy("d3", zz, z, d3s.at[zz], d3r.at[z], row_of(zz, xl, c), rep).start()

    loop(1, n, d3_step)
    d3o[...] = d3_sum(z)

    def a3_step(o):
        zz = around(z, o)
        arrived("a3", zz, a2_like)
        pass_core((1 - xl) * n + zz)

    loop(0, n, a3_step)

    def d3_add(o):
        zz = around(z, o)
        arrived("d3", zz, d3r.at[zz])
        d3o[...] += d3r[zz].astype(F32)

    loop(1, n, d3_add)
    d4s[...] = d3o[...].astype(BF)
    for k in range(2):
        same = is_me(owner_rows[k], owner_rep)
        src, dst = d4s.at[k], gc.at[owner_rep, own_half]

        @pl.when(jnp.logical_not(same))
        def _(src=src, dst=dst, k=k):
            copy("d4", k, own_half, src, dst, owner_rows[k], owner_rep).start()

        @pl.when(same)
        def _(src=src, dst=dst):
            pltpu.make_async_copy(src, dst, recv.at[places["d4"] + own_half]).start()

    loop(0, 2 * n, lambda m: arrived("a4", m, a2_like))

    for t in range(tiles):
        _, _, kt, jt = picks[t]
        rs[t] = pj[pl.ds(jt * ppt, ppt), kt].reshape(side, width)

    chunks_pair = 2 * side // (2 * piece_rows)
    pairs_half = block // 2 // (2 * side)

    def forward_pair(u):
        for h in range(2):
            for t in range(tiles):
                live, it, _, _ = picks[t]
                cond = jnp.logical_and(live, it == 2 * u + h)
                lhs[h * side:(h + 1) * side, t * side:(t + 1) * side] = chosen(cond, mk[t])
        total = jnp.dot(lhs[...], rs[...].reshape(tiles * side, width), preferred_element_type=F32)
        yb[pl.ds(u * chunks_pair, chunks_pair)] = total.astype(BF).reshape(
            chunks_pair, 2 * piece_rows, width
        )

    loop(0, pairs_half, lambda i: forward_pair((1 - xh) * pairs_half + i))

    def c1_step(o):
        yy = around(y, o)
        copy("c1", yy, yy, yb.at[(1 - xh) * n + yy], c1r.at[yy], row, hi_rep).start()

    loop(1, n + 1, c1_step)
    loop(0, pairs_half, lambda i: forward_pair(xh * pairs_half + i))

    def pass_hi(name, ref, yy):
        at = xh * n + yy
        copy(name, yy, yy, ref.at[at], ref.at[at], row, hi_rep).start()

    def pass_y(name, ref, o):
        yy = around(y, o)
        copy(name, yy, y, ref.at[rep], ref.at[rep], row, xh * n + yy).start()

    arrived("d4", 0, d4s.at[0])
    arrived("d4", 1, d4s.at[0])
    pass_hi("d6", gc, y)
    loop(1, n, lambda o: pass_y("d5", gc, o))

    def c2_sum(yy):
        arrived("c1", yy, c1r.at[yy])
        return yb[xh * n + yy].astype(F32) + c1r[yy].astype(F32)

    def c2_step(o):
        yy = around(y, o)
        c2s[yy] = c2_sum(yy).astype(BF)
        copy("c2", yy, y, c2s.at[yy], c2r.at[y], row, xh * n + yy).start()

    loop(1, n, c2_step)
    c2o[...] = c2_sum(y)

    def relay(got, gone, ref, o):
        yy = around(y, o)
        arrived(got, yy, ref.at[rep])
        pass_hi(gone, ref, yy)

    loop(1, n, lambda o: relay("d5", "d6", gc, o))

    def c2_add(o):
        yy = around(y, o)
        arrived("c2", yy, c2r.at[yy])
        c2o[...] += c2r[yy].astype(F32)

    loop(1, n, c2_add)
    oc[rep] = c2o[...].astype(BF)
    pass_hi("c4", oc, y)
    loop(1, n, lambda o: pass_y("c3", oc, o))

    for t in range(tiles):
        live = picks[t][0]
        scores = lax.dot_general(gs[t], rs[t], (((1,), (1,)), ((), ())), preferred_element_type=F32)
        ge[t] = chosen(live, tv[t].astype(F32) * scores)
    outs = [pltpu.make_async_copy(ge, ge_h, local.at[0])]
    outs[-1].start()
    cpt = side // (2 * piece_rows)
    for i in range(per_side):
        rows = feats[i * cpt:(i + 1) * cpt].reshape(side, width)
        ft[:, i * side:(i + 1) * side] = rows.astype(F32).T.astype(BF)

    loop(0, n, lambda yy: arrived("d6", yy, gc.at[rep]))
    grad_cols = gc[...].reshape(block, width)
    wp[...] = jnp.dot(ft[...], grad_cols, preferred_element_type=F32).reshape(wp.shape)
    wz[z] = wp[rep]

    def wz_step(o):
        zz = around(z, o)
        copy("wz", zz, z, wz.at[z], wz.at[z], row_of(zz, xl, c), rep).start()

    loop(1, n, wz_step)
    loop(1, n, lambda o: relay("c3", "c4", oc, o))

    fg[...] = lax.dot_general(
        gc[...].reshape(block, width), weff[...], (((1,), (1,)), ((), ())), preferred_element_type=F32
    ).astype(BF)
    outs.append(pltpu.make_async_copy(fg, fg_h, local.at[1]))
    outs[-1].start()

    loop(1, n, lambda o: arrived("wz", around(z, o), wz.at[z]))
    spot = xl * 2 + c
    wc[spot] = functools.reduce(jnp.add, [wz[i] for i in range(n)])
    for i, (r, s) in enumerate(
        ((core_row, xl * 2 + 1 - c), (lo_row, (1 - xl) * 2 + c), (both_row, (1 - xl) * 2 + 1 - c))
    ):
        copy("wc", s, spot, wc.at[spot], wc.at[spot], r, rep).start()

    loop(0, n, lambda yy: arrived("c4", yy, oc.at[rep]))
    outs.append(pltpu.make_async_copy(oc, out_h, local.at[2]))
    outs[-1].start()

    for i in range(1, 4):
        arrived("wc", lax.rem(spot + i, 4), wc.at[spot])
    wa[rep] = (wc[0] + wc[1]) + (wc[2] + wc[3])
    pass_hi("wx", wa, y)
    loop(1, n, lambda o: pass_y("wy", wa, o))
    loop(1, n, lambda o: relay("wy", "wx", wa, o))
    loop(0, n, lambda yy: arrived("wx", yy, wa.at[rep]))
    wgo[...] = jnp.where(wm[...] != 0, wa[...].reshape(width, width), 0.0)
    outs.append(pltpu.make_async_copy(wgo, wg_h, local.at[3]))
    outs[-1].start()

    for k in range(2):
        pl.when(jnp.logical_not(is_me(part_rows[k], group)))(functools.partial(left, "a1", k, a1s.at[0]))
        pl.when(jnp.logical_not(is_me(owner_rows[k], owner_rep)))(
            functools.partial(left, "d4", k, d4s.at[0])
        )

    def along_z(o):
        zz = around(z, o)
        left("a2", zz, a2_like)
        left("d3", zz, a2_like)
        left("wz", zz, wz.at[z])

    def along_y(o):
        yy = around(y, o)
        left("d5", yy, gc.at[rep])
        left("c2", yy, oc.at[rep])
        left("c3", yy, oc.at[rep])
        left("wy", yy, wa.at[rep])

    def across(i):
        left("a3", i, a2_like)
        left("d2", i, a2_like)
        left("d6", i, gc.at[rep])
        left("c1", i, oc.at[rep])
        left("c4", i, oc.at[rep])
        left("wx", i, wa.at[rep])

    def cores(m):
        left("a4", m, a2_like)
        left("d1", m, a2_like)

    loop(1, n, along_z)
    loop(1, n, along_y)
    loop(0, n, across)
    loop(0, 2 * n, cores)
    for i in range(1, 4):
        left("wc", lax.rem(spot + i, 4), wc.at[spot])
    for out in outs:
        out.wait()


def on_device(feats, weight, weight_mask, tile_vals, edge_mask, tile_pos, grad_out):
    reps = lax.axis_size("rep")
    n = reps // 2
    block, width = feats.shape
    tiles, side, _ = tile_vals.shape
    rows = block // (4 * n)
    share = width // reps
    places, total = semaphore_places(n)
    chunked = (reps, 2 * rows, width)
    piece = (2, rows, width)

    def vm(shape, kind=BF):
        return pltpu.VMEM(shape, kind)

    scratch = [
        vm(chunked), vm((block // side, side, width)), vm((width, width)), vm((width, width), jnp.int32),
        vm((tiles, side, side)), vm((tiles, side, side), F32),
        vm((width, width)), vm(piece), vm((4 * n,) + piece),
        vm((tiles, side, side)), vm((tiles, side, side)),
        vm((tiles, side, width)), vm((tiles, side, width)),
        vm((2 * side, tiles * side)), vm((4 * n,) + piece),
        vm((2 * n,) + piece), vm((n,) + piece), vm((n,) + piece), vm((n,) + piece), vm((n,) + piece),
        vm(piece, F32), vm(piece), vm((reps,) + piece),
        vm(chunked), vm((n,) + chunked[1:]), vm((n,) + chunked[1:]), vm((n,) + chunked[1:]),
        vm(chunked[1:], F32), vm(chunked),
        vm((width, block)), vm((reps, share, width), F32), vm((n, share, width), F32),
        vm((4, share, width), F32), vm((reps, share, width), F32), vm((width, width), F32),
        vm((tiles, side, side), F32), vm((block, width)),
        pltpu.SemaphoreType.DMA((total,)), pltpu.SemaphoreType.DMA((total,)),
        pltpu.SemaphoreType.DMA((6,)),
    ]
    anywhere = pl.BlockSpec(memory_space=pl.ANY)
    out, fgrad, wgrad, edge = pl.pallas_call(
        functools.partial(kernel, n, places),
        out_shape=(
            jax.ShapeDtypeStruct(chunked, BF),
            jax.ShapeDtypeStruct((block, width), BF),
            jax.ShapeDtypeStruct((width, width), F32),
            jax.ShapeDtypeStruct((tiles, side, side), F32),
        ),
        in_specs=[pl.BlockSpec(memory_space=pltpu.SMEM)] + [anywhere] * 6,
        out_specs=(anywhere,) * 4,
        scratch_shapes=scratch,
        compiler_params=pltpu.CompilerParams(
            collective_id=0, has_side_effects=True, vmem_limit_bytes=40 * 1024 * 1024
        ),
        cost_estimate=pl.CostEstimate(
            flops=3_000_000_000, bytes_accessed=5_000_000, transcendentals=0
        ),
        name="layer",
    )(
        tile_pos,
        feats.reshape(chunked),
        grad_out.reshape(block // side, side, width),
        weight,
        weight_mask,
        tile_vals,
        edge_mask,
    )
    return out.reshape(block, width), fgrad, wgrad, edge


def solution(mesh):
    placed = (
        P("row", None),
        P(),
        P(),
        P(("row", "rep"), None, None),
        P(("row", "rep"), None, None),
        P(("row", "rep")),
        P("row", None),
    )
    return jax.shard_map(
        on_device,
        mesh=mesh,
        in_specs=placed,
        out_specs=(P("row", None), P("row", None), P(), P(("row", "rep"), None, None)),
        check_vma=False,
    )
```

```python
import functools

import jax
import jax.numpy as jnp
from jax import lax
from jax.experimental import pallas as pl
from jax.experimental.pallas import tpu as pltpu
from jax.sharding import PartitionSpec as P

BF = jnp.bfloat16
F32 = jnp.float32
VMEM_MIB = 56


def semaphore_places(n):
    counts = dict(
        a1=n, a3=n, a4=2 * n,
        d1=n, d2=n // 2, d3=n, d5=n, d6=n,
        c1=n, c2=n, c3=n, c4=n,
        wx=8, wz=n, wy=n, wa=n, wb=8,
    )
    places, total = {}, 0
    for name, count in counts.items():
        places[name] = total
        total += count
    return places, total


def loop(low, high, step):
    def run(i, carry):
        step(i)
        return carry

    lax.fori_loop(low, high, run, 0)


def kernel(
    n, places,
    pos_ref, feats_h, gout_h, w_h, wm_h, tv_h, em_h,
    out_h, fg_h, wg_h, ge_h,
    chunk, gout, w, wm, tv, em,
    weff, pj, mk, mkt, gs, rsf, rs, lhs, pb,
    d1r, d2s, d2r, d3s, d3r, gc,
    yb, c1r, c2s, c2r, c2o, oc,
    wl, wxs, wxr, wzs, wzr, wyr, wag, wgo, ge, fg,
    send, recv, local,
):
    row, rep = lax.axis_index("row"), lax.axis_index("rep")
    z, xl, c = row // 4, row // 2 % 2, row % 2
    xh, y = rep // n, rep % n
    reps = 2 * n
    half = n // 2
    tiles, side, _ = tv.shape
    width = w.shape[0]
    chunk_rows = chunk.shape[0]
    per_side = gout.shape[0]
    cpt = side // chunk_rows
    block = per_side * side
    spot = xh * 4 + xl * 2 + c

    def row_of(zz, xx, cc):
        return zz * 4 + xx * 2 + cc

    core_row, lo_row = row_of(z, xl, 1 - c), row_of(z, 1 - xl, c)
    hi_rep = (1 - xh) * n + y
    quarter = (c * 2 + xl) * half
    section, group = row // reps, lax.rem(row, reps)

    def around(at, o):
        return lax.rem(at + o, n)

    def copy(name, i, j, src, dst, to_row, to_rep):
        return pltpu.make_async_remote_copy(
            src_ref=src,
            dst_ref=dst,
            send_sem=send.at[places[name] + i],
            recv_sem=recv.at[places[name] + j],
            device_id=(to_row, to_rep),
            device_id_type=pl.DeviceIdType.MESH,
        )

    def arrived(name, j, ref):
        copy(name, 0, j, ref, ref, core_row, rep).wait_recv()

    def left(name, i, ref):
        copy(name, i, 0, ref, ref, core_row, rep).wait_send()

    def owner(k, i):
        return k * reps + rep, quarter + i

    def reader(zz):
        return row_of(zz, y // half, xh), group

    def line(s):
        return row_of(z, lax.rem(s // 2, 2), lax.rem(s, 2)), s // 4 * n + y

    def is_me(r, q):
        return jnp.logical_and(r == row, q == rep)

    def send_or_keep(name, i, j, src, dst, r, q):
        same = is_me(r, q)

        @pl.when(jnp.logical_not(same))
        def _():
            copy(name, i, j, src, dst, r, q).start()

        @pl.when(same)
        def _():
            pltpu.make_async_copy(src, dst, recv.at[places[name] + j]).start()

    ins = []
    for i, (src, dst) in enumerate(
        ((feats_h.at[rep], chunk), (tv_h, tv), (em_h, em), (gout_h, gout), (w_h, w), (wm_h, wm))
    ):
        ins.append(pltpu.make_async_copy(src, dst, local.at[i]))
        ins[-1].start()

    barrier = pltpu.get_barrier_semaphore()

    def greet(r, q):
        pl.semaphore_signal(barrier, inc=1, device_id=(r, q), device_id_type=pl.DeviceIdType.MESH)

    def greet_other(r, q):
        pl.when(jnp.logical_not(is_me(r, q)))(functools.partial(greet, r, q))

    loop(0, n, lambda i: greet_other(*reader(i)))
    loop(0, n, lambda m: greet_other(*owner(m // half, lax.rem(m, half))))
    loop(1, 8, lambda o: greet(*line(lax.rem(spot + o, 8))))
    loop(1, n, lambda o: greet(row_of(around(z, o), xl, c), rep))
    loop(1, n, lambda o: greet(row, xh * n + around(y, o)))
    same = jnp.logical_and(group == rep, jnp.logical_and(y // half == xl, xh == c))
    expected = 7 + 2 * (n - 1) + 2 * n - 2 * same.astype(jnp.int32)

    ins[0].wait()
    pl.semaphore_wait(barrier, expected)

    def a1_step(o):
        zz = around(z, o)
        r, q = reader(zz)
        send_or_keep("a1", zz, section * half + lax.rem(rep, half), chunk, pj.at[rep, section], r, q)

    loop(0, n, a1_step)

    picks = []
    for t in range(tiles):
        pos = pos_ref[t]
        slot = jnp.maximum(pos, 0)
        picks.append(
            (
                pos >= 0,
                lax.rem(slot // per_side, per_side),
                slot // (per_side * per_side),
                lax.rem(slot, per_side),
            )
        )

    ins[1].wait()
    ins[2].wait()
    ins[3].wait()
    for t in range(tiles):
        product = tv[t].astype(F32) * em[t]
        mk[t] = product.astype(BF)
        mkt[t] = product.T.astype(BF)
        gs[t] = gout[picks[t][1]]

    def chosen(cond, tile):
        return lax.select_n(cond, jnp.zeros_like(tile), tile)

    def backward_tile(jj):
        for k in range(2):
            for t in range(tiles):
                live, _, kt, jt = picks[t]
                cond = jnp.logical_and(live, jnp.logical_and(kt == k, jt == jj))
                lhs[k * side:(k + 1) * side, t * side:(t + 1) * side] = chosen(cond, mkt[t])
        total = jnp.dot(lhs[...], gs[...].reshape(tiles * side, width), preferred_element_type=F32)
        total = total.astype(BF)
        for k in range(2):
            pb[pl.ds(jj * cpt, cpt), k] = total[k * side:(k + 1) * side].reshape(cpt, chunk_rows, width)

    quarter_tiles = half // cpt

    def send_quarter(x):
        def one(i):
            m = x * half + i
            copy("d1", m, m, pb.at[(1 - c) * n + m], d1r.at[m], core_row, rep).start()

        first = ((1 - c) * 2 + x) * quarter_tiles
        loop(0, quarter_tiles, lambda i: backward_tile(first + i))
        loop(0, half, one)

    send_quarter(1 - xl)
    send_quarter(xl)
    loop(0, 2 * quarter_tiles, lambda i: backward_tile(c * 2 * quarter_tiles + i))

    def d2_step(o):
        i = lax.rem(z + o, half)
        m = (1 - xl) * half + i
        arrived("d1", m, d1r.at[m])
        d2s[i] = (pb[c * n + m].astype(F32) + d1r[m].astype(F32)).astype(BF)
        copy("d2", i, i, d2s.at[i], d2r.at[i], lo_row, rep).start()

    loop(0, half, d2_step)

    def chunk_of(x, m):
        return pj.at[(c * 2 + x) * half + lax.rem(m, half), m // half]

    def pass_core(x, m):
        ref = chunk_of(x, m)
        copy("a4", x * n + m, x * n + m, ref, ref, core_row, rep).start()

    def a1_arrival(m):
        ref = chunk_of(xl, m)
        arrived("a1", m, chunk)
        copy("a3", m, m, ref, ref, lo_row, rep).start()
        pass_core(xl, m)

    loop(0, n, a1_arrival)

    def d3_step(o):
        i = lax.rem(z + o, half)
        m = xl * half + i
        arrived("d1", m, d1r.at[m])
        arrived("d2", i, d2r.at[i])
        total = pb[c * n + m].astype(F32) + d1r[m].astype(F32) + d2r[i].astype(F32)
        d3s[i] = total.astype(BF)
        for k in range(2):
            r, q = owner(k, i)
            send_or_keep("d3", k * half + i, z, d3s.at[i, k], d3r.at[z], r, q)

    loop(0, half, d3_step)

    def a3_arrival(m):
        arrived("a3", m, chunk)
        pass_core(1 - xl, m)

    loop(0, n, a3_arrival)
    ins[4].wait()
    ins[5].wait()
    weff[...] = jnp.where(wm[...] != 0, w[...].astype(F32), 0.0).astype(BF)
    loop(0, 2 * n, lambda m: arrived("a4", m, chunk))

    for t in range(tiles):
        _, _, kt, jt = picks[t]
        rsf[t] = pj[pl.ds(jt * cpt, cpt), kt].reshape(side, width)
    rs[...] = (
        jnp.dot(rsf[...].reshape(tiles * side, width), weff[...], preferred_element_type=F32)
        .astype(BF)
        .reshape(tiles, side, width)
    )

    chunks_pair = 2 * side // chunk_rows
    pairs_half = block // 2 // (2 * side)

    def forward_pair(u):
        for h in range(2):
            for t in range(tiles):
                live, it, _, _ = picks[t]
                cond = jnp.logical_and(live, it == 2 * u + h)
                lhs[h * side:(h + 1) * side, t * side:(t + 1) * side] = chosen(cond, mk[t])
        total = jnp.dot(lhs[...], rs[...].reshape(tiles * side, width), preferred_element_type=F32)
        yb[pl.ds(u * chunks_pair, chunks_pair)] = total.astype(BF).reshape(
            chunks_pair, chunk_rows, width
        )

    loop(0, pairs_half, lambda i: forward_pair((1 - xh) * pairs_half + i))

    def c1_step(o):
        yy = around(y, o)
        copy("c1", yy, yy, yb.at[(1 - xh) * n + yy], c1r.at[yy], row, hi_rep).start()

    loop(1, n + 1, c1_step)

    wl[...] = jnp.zeros_like(wl)
    deep = max(1, 256 // (2 * chunk_rows))

    def weight_step(i):
        at = pl.ds(i * deep, deep)
        left_side = pj[at].reshape(2 * deep * chunk_rows, width)
        right_side = pb[at].reshape(2 * deep * chunk_rows, width)
        wl[...] += lax.dot_general(
            left_side, right_side, (((0,), (0,)), ((), ())), preferred_element_type=F32
        ).reshape(wl.shape)

    loop(0, reps // deep, weight_step)
    wxs[...] = wl[...].astype(BF)

    def wx_step(o):
        s = lax.rem(spot + o, 8)
        r, q = line(s)
        copy("wx", s, spot, wxs.at[s], wxr.at[spot], r, q).start()

    loop(1, 8, wx_step)
    loop(0, pairs_half, lambda i: forward_pair(xh * pairs_half + i))

    def pass_hi(name, ref, yy):
        at = xh * n + yy
        copy(name, yy, yy, ref.at[at], ref.at[at], row, hi_rep).start()

    def pass_y(name, ref, o):
        yy = around(y, o)
        copy(name, yy, y, ref.at[rep], ref.at[rep], row, xh * n + yy).start()

    loop(0, n, lambda i: arrived("d3", i, chunk))
    gc[rep] = functools.reduce(jnp.add, [d3r[i].astype(F32) for i in range(n)]).astype(BF)
    pass_hi("d6", gc, y)
    loop(1, n, lambda o: pass_y("d5", gc, o))

    def c2_sum(yy):
        arrived("c1", yy, chunk)
        return yb[xh * n + yy].astype(F32) + c1r[yy].astype(F32)

    def c2_step(o):
        yy = around(y, o)
        c2s[yy] = c2_sum(yy).astype(BF)
        copy("c2", yy, y, c2s.at[yy], c2r.at[y], row, xh * n + yy).start()

    loop(1, n, c2_step)
    c2o[...] = c2_sum(y)

    share = wl.shape[1]
    tall = share * 2 // n

    def wx_arrival(o):
        s = lax.rem(spot + o, 8)
        arrived("wx", s, wxr.at[s])
        wl[spot] += wxr[s].astype(F32)

    loop(1, 8, wx_arrival)
    mine = wl[spot]
    for i in range(n):
        g, h = i // 2, i % 2
        wzs[i] = mine[g * tall:(g + 1) * tall, h * 128:(h + 1) * 128]

    def wz_step(o):
        zz = around(z, o)
        copy("wz", zz, z, wzs.at[zz], wzr.at[z], row_of(zz, xl, c), rep).start()

    loop(1, n, wz_step)

    def relay(got, gone, ref, o):
        yy = around(y, o)
        arrived(got, yy, chunk)
        pass_hi(gone, ref, yy)

    loop(1, n, lambda o: relay("d5", "d6", gc, o))

    def c2_add(o):
        yy = around(y, o)
        arrived("c2", yy, chunk)
        c2o[...] += c2r[yy].astype(F32)

    loop(1, n, c2_add)
    oc[rep] = c2o[...].astype(BF)
    pass_hi("c4", oc, y)
    loop(1, n, lambda o: pass_y("c3", oc, o))

    def wz_arrival(o):
        zz = around(z, o)
        arrived("wz", zz, wzr.at[zz])
        wzs[z] += wzr[zz]

    loop(1, n, wz_arrival)
    wyr[y] = wzs[z]

    def wy_step(o):
        yy = around(y, o)
        copy("wy", yy, y, wyr.at[y], wyr.at[y], row, xh * n + yy).start()

    loop(1, n, wy_step)

    for t in range(tiles):
        live = picks[t][0]
        scores = lax.dot_general(gs[t], rs[t], (((1,), (1,)), ((), ())), preferred_element_type=F32)
        ge[t] = chosen(live, tv[t].astype(F32) * scores)
    outs = [pltpu.make_async_copy(ge, ge_h, local.at[0])]
    outs[-1].start()

    loop(1, n, lambda o: arrived("wy", around(y, o), wyr.at[y]))
    wag[spot, z] = functools.reduce(jnp.add, [wyr[i] for i in range(n)])

    def wa_step(o):
        zz = around(z, o)
        copy("wa", zz, z, wag.at[spot, z], wag.at[spot, z], row_of(zz, xl, c), rep).start()

    loop(1, n, wa_step)
    loop(1, n, lambda o: relay("c3", "c4", oc, o))

    loop(0, n, lambda yy: arrived("d6", yy, chunk))
    fg[...] = lax.dot_general(
        gc[...].reshape(block, width), weff[...], (((1,), (1,)), ((), ())), preferred_element_type=F32
    ).astype(BF)
    outs.append(pltpu.make_async_copy(fg, fg_h, local.at[1]))
    outs[-1].start()

    loop(1, n, lambda o: arrived("wa", around(z, o), wyr.at[y]))

    def wb_step(o):
        s = lax.rem(spot + o, 8)
        r, q = line(s)
        copy("wb", s, spot, wag.at[spot], wag.at[spot], r, q).start()

    loop(1, 8, wb_step)

    loop(0, n, lambda yy: arrived("c4", yy, chunk))
    outs.append(pltpu.make_async_copy(oc, out_h, local.at[2]))
    outs[-1].start()

    loop(1, 8, lambda o: arrived("wb", lax.rem(spot + o, 8), wag.at[spot]))
    for s in range(8):
        for i in range(n):
            g, h = i // 2, i % 2
            top = s * share + g * tall
            at = (slice(top, top + tall), slice(h * 128, (h + 1) * 128))
            wgo[at] = jnp.where(wm[at] != 0, wag[s, i], 0.0)
    outs.append(pltpu.make_async_copy(wgo, wg_h, local.at[3]))
    outs[-1].start()

    def left_if_sent(name, i, r, q):
        pl.when(jnp.logical_not(is_me(r, q)))(functools.partial(left, name, i, chunk))

    loop(0, n, lambda i: left_if_sent("a1", i, *reader(i)))
    loop(0, n, lambda m: left_if_sent("d3", m, *owner(m // half, lax.rem(m, half))))

    def along(o):
        zz, yy = around(z, o), around(y, o)
        left("wz", zz, wyr.at[y])
        left("wa", zz, wyr.at[y])
        left("wy", yy, wyr.at[y])
        left("d5", yy, chunk)
        left("c2", yy, chunk)
        left("c3", yy, chunk)

    def across(i):
        left("a3", i, chunk)
        left("d1", i, d1r.at[0])
        left("d6", i, chunk)
        left("c1", i, chunk)
        left("c4", i, chunk)
        left("a4", i, chunk)
        left("a4", n + i, chunk)

    def over_line(o):
        s = lax.rem(spot + o, 8)
        left("wx", s, wxs.at[s])
        left("wb", s, wag.at[spot])

    loop(1, n, along)
    loop(0, n, across)
    loop(0, half, lambda i: left("d2", i, d1r.at[0]))
    loop(1, 8, over_line)
    for out in outs:
        out.wait()


def settle_kernel(*refs):
    pairs, sem = list(zip(refs[:4], refs[4:8])), refs[8]
    copies = [pltpu.make_async_copy(src, dst, sem.at[i]) for i, (src, dst) in enumerate(pairs)]
    for one in copies:
        one.start()
    for one in copies:
        one.wait()


def settle(*arrays):
    anywhere = pl.BlockSpec(memory_space=pl.ANY)
    return pl.pallas_call(
        settle_kernel,
        out_shape=tuple(jax.ShapeDtypeStruct(a.shape, a.dtype) for a in arrays),
        in_specs=[anywhere] * 4,
        out_specs=(anywhere,) * 4,
        scratch_shapes=[pltpu.SemaphoreType.DMA((4,))],
        compiler_params=pltpu.CompilerParams(vmem_limit_bytes=VMEM_MIB * 1024 * 1024),
        name="settle",
    )(*arrays)


def on_device(feats, weight, weight_mask, tile_vals, edge_mask, tile_pos, grad_out):
    reps = lax.axis_size("rep")
    n = reps // 2
    block, width = feats.shape
    tiles, side, _ = tile_vals.shape
    rows = block // reps
    share = width // 8
    tall = share * 2 // n
    places, total = semaphore_places(n)
    chunked = (reps, rows, width)
    pair = (2, rows, width)

    def vm(shape, kind=BF):
        return pltpu.VMEM(shape, kind)

    scratch = [
        vm(chunked[1:]), vm((block // side, side, width)), vm((width, width)), vm((width, width), jnp.int32),
        vm((tiles, side, side)), vm((tiles, side, side), F32),
        vm((width, width)), vm((reps,) + pair),
        vm((tiles, side, side)), vm((tiles, side, side)),
        vm((tiles, side, width)), vm((tiles, side, width)), vm((tiles, side, width)),
        vm((2 * side, tiles * side)), vm((reps,) + pair),
        vm((n,) + pair), vm((n // 2,) + pair), vm((n // 2,) + pair), vm((n // 2,) + pair),
        vm((n,) + chunked[1:]), vm(chunked),
        vm(chunked), vm((n,) + chunked[1:]), vm((n,) + chunked[1:]), vm((n,) + chunked[1:]),
        vm(chunked[1:], F32), vm(chunked),
        vm((8, share, width), F32), vm((8, share, width)), vm((8, share, width)),
        vm((n, tall, 128), F32), vm((n, tall, 128), F32), vm((n, tall, 128), F32),
        vm((8, n, tall, 128), F32), vm((width, width), F32),
        vm((tiles, side, side), F32), vm((block, width)),
        pltpu.SemaphoreType.DMA((total,)), pltpu.SemaphoreType.DMA((total,)),
        pltpu.SemaphoreType.DMA((6,)),
    ]
    anywhere = pl.BlockSpec(memory_space=pl.ANY)
    out, fgrad, wgrad, edge = pl.pallas_call(
        functools.partial(kernel, n, places),
        out_shape=(
            jax.ShapeDtypeStruct(chunked, BF),
            jax.ShapeDtypeStruct((block, width), BF),
            jax.ShapeDtypeStruct((width, width), F32),
            jax.ShapeDtypeStruct((tiles, side, side), F32),
        ),
        in_specs=[pl.BlockSpec(memory_space=pltpu.SMEM)] + [anywhere] * 6,
        out_specs=(anywhere,) * 4,
        scratch_shapes=scratch,
        compiler_params=pltpu.CompilerParams(
            collective_id=0, has_side_effects=True, vmem_limit_bytes=VMEM_MIB * 1024 * 1024
        ),
        cost_estimate=pl.CostEstimate(
            flops=3_000_000_000, bytes_accessed=5_000_000, transcendentals=0
        ),
        name="layer",
    )(
        tile_pos,
        feats.reshape(chunked),
        grad_out.reshape(block // side, side, width),
        weight,
        weight_mask,
        tile_vals,
        edge_mask,
    )
    return settle(out.reshape(block, width), fgrad, wgrad, edge)


def solution(mesh):
    placed = (
        P("row", None),
        P(),
        P(),
        P(("row", "rep"), None, None),
        P(("row", "rep"), None, None),
        P(("row", "rep")),
        P("row", None),
    )
    return jax.shard_map(
        on_device,
        mesh=mesh,
        in_specs=placed,
        out_specs=(P("row", None), P("row", None), P(), P(("row", "rep"), None, None)),
        check_vma=False,
    )
```

```python
import functools

import jax
import jax.numpy as jnp
from jax import lax
from jax.experimental import pallas as pl
from jax.experimental.pallas import tpu as pltpu
from jax.sharding import PartitionSpec as P

BF = jnp.bfloat16
F32 = jnp.float32
VMEM_MIB = 56


def doublings(n):
    return n.bit_length() - 1


def semaphore_places(n):
    counts = dict(
        a1=n, a3=n, a4=2 * n,
        d1=n, d2=n // 2, d3=n, d5=n, d6=n,
        c1=n, c2=n, c3=n, c4=n,
        w5=2 + doublings(n),
    )
    places, total = {}, 0
    for name, count in counts.items():
        places[name] = total
        total += count
    return places, total


def loop(low, high, step):
    def run(i, carry):
        step(i)
        return carry

    lax.fori_loop(low, high, run, 0)


def kernel(
    n, places,
    pos_ref, feats_h, gout_h, w_h, wm_h, tv_h, em_h,
    out_h, fg_h, wg_h, ge_h,
    chunk, gout, w, wm, tv, em,
    weff, pj, mk, mkt, gs, rsf, rs, lhs, pb,
    d1r, d2s, d2r, d3s, d3r, gc,
    yb, c1r, c2s, c2r, c2o, oc,
    wl, w5s, w5r, wgo, ge, fg,
    send, recv, local, round_y, round_x,
):
    row, rep = lax.axis_index("row"), lax.axis_index("rep")
    z, xl, c = row // 4, row // 2 % 2, row % 2
    xh, y = rep // n, rep % n
    reps = 2 * n
    half = n // 2
    tiles, side, _ = tv.shape
    width = w.shape[0]
    chunk_rows = chunk.shape[0]
    per_side = gout.shape[0]
    cpt = side // chunk_rows
    block = per_side * side
    spot = xh * 4 + xl * 2 + c

    def row_of(zz, xx, cc):
        return zz * 4 + xx * 2 + cc

    core_row, lo_row = row_of(z, xl, 1 - c), row_of(z, 1 - xl, c)
    hi_rep = (1 - xh) * n + y
    quarter = (c * 2 + xl) * half
    section, group = row // reps, lax.rem(row, reps)

    def around(at, o):
        return lax.rem(at + o, n)

    def copy(name, i, j, src, dst, to_row, to_rep):
        return pltpu.make_async_remote_copy(
            src_ref=src,
            dst_ref=dst,
            send_sem=send.at[places[name] + i],
            recv_sem=recv.at[places[name] + j],
            device_id=(to_row, to_rep),
            device_id_type=pl.DeviceIdType.MESH,
        )

    def arrived(name, j, ref):
        copy(name, 0, j, ref, ref, core_row, rep).wait_recv()

    def left(name, i, ref):
        copy(name, i, 0, ref, ref, core_row, rep).wait_send()

    def owner(k, i):
        return k * reps + rep, quarter + i

    def reader(zz):
        return row_of(zz, y // half, xh), group

    def line(s):
        return row_of(z, lax.rem(s // 2, 2), lax.rem(s, 2)), s // 4 * n + y

    def is_me(r, q):
        return jnp.logical_and(r == row, q == rep)

    def send_or_keep(name, i, j, src, dst, r, q):
        same = is_me(r, q)

        @pl.when(jnp.logical_not(same))
        def _():
            copy(name, i, j, src, dst, r, q).start()

        @pl.when(same)
        def _():
            pltpu.make_async_copy(src, dst, recv.at[places[name] + j]).start()

    ins = []
    for i, (src, dst) in enumerate(
        ((feats_h.at[rep], chunk), (tv_h, tv), (em_h, em), (gout_h, gout), (w_h, w), (wm_h, wm))
    ):
        ins.append(pltpu.make_async_copy(src, dst, local.at[i]))
        ins[-1].start()

    barrier = pltpu.get_barrier_semaphore()

    def greet(r, q):
        pl.semaphore_signal(barrier, inc=1, device_id=(r, q), device_id_type=pl.DeviceIdType.MESH)

    def greet_line(sem):
        def one(o):
            r, q = line(lax.rem(spot + o, 8))
            pl.semaphore_signal(sem, inc=1, device_id=(r, q), device_id_type=pl.DeviceIdType.MESH)

        loop(1, 8, one)

    def greet_y(sem):
        def one(o):
            q = xh * n + around(y, o)
            pl.semaphore_signal(sem, inc=1, device_id=(row, q), device_id_type=pl.DeviceIdType.MESH)

        loop(1, n, one)

    loop(1, n, lambda o: greet(row_of(around(z, o), xl, c), rep))
    greet_y(barrier)
    greet_line(barrier)
    pl.semaphore_wait(barrier, 7 + 2 * (n - 1))
    greet_y(round_y)
    pl.semaphore_wait(round_y, n - 1)
    greet_line(round_x)
    pl.semaphore_wait(round_x, 7)

    ins[0].wait()

    def a1_step(o):
        zz = around(z, o)
        r, q = reader(zz)
        send_or_keep("a1", zz, section * half + lax.rem(rep, half), chunk, pj.at[rep, section], r, q)

    loop(0, n, a1_step)

    picks = []
    for t in range(tiles):
        pos = pos_ref[t]
        slot = jnp.maximum(pos, 0)
        picks.append(
            (
                pos >= 0,
                lax.rem(slot // per_side, per_side),
                slot // (per_side * per_side),
                lax.rem(slot, per_side),
            )
        )

    ins[1].wait()
    ins[2].wait()
    ins[3].wait()
    for t in range(tiles):
        product = tv[t].astype(F32) * em[t]
        mk[t] = product.astype(BF)
        mkt[t] = product.T.astype(BF)
        gs[t] = gout[picks[t][1]]

    def chosen(cond, tile):
        return lax.select_n(cond, jnp.zeros_like(tile), tile)

    def backward_tile(jj):
        for k in range(2):
            for t in range(tiles):
                live, _, kt, jt = picks[t]
                cond = jnp.logical_and(live, jnp.logical_and(kt == k, jt == jj))
                lhs[k * side:(k + 1) * side, t * side:(t + 1) * side] = chosen(cond, mkt[t])
        total = jnp.dot(lhs[...], gs[...].reshape(tiles * side, width), preferred_element_type=F32)
        total = total.astype(BF)
        for k in range(2):
            pb[pl.ds(jj * cpt, cpt), k] = total[k * side:(k + 1) * side].reshape(cpt, chunk_rows, width)

    quarter_tiles = half // cpt

    def send_quarter(x):
        def one(i):
            m = x * half + i
            copy("d1", m, m, pb.at[(1 - c) * n + m], d1r.at[m], core_row, rep).start()

        first = ((1 - c) * 2 + x) * quarter_tiles
        loop(0, quarter_tiles, lambda i: backward_tile(first + i))
        loop(0, half, one)

    send_quarter(1 - xl)
    send_quarter(xl)
    loop(0, 2 * quarter_tiles, lambda i: backward_tile(c * 2 * quarter_tiles + i))

    def d2_step(o):
        i = lax.rem(z + o, half)
        m = (1 - xl) * half + i
        arrived("d1", m, d1r.at[m])
        d2s[i] = (pb[c * n + m].astype(F32) + d1r[m].astype(F32)).astype(BF)
        copy("d2", i, i, d2s.at[i], d2r.at[i], lo_row, rep).start()

    loop(0, half, d2_step)

    def chunk_of(x, m):
        return pj.at[(c * 2 + x) * half + lax.rem(m, half), m // half]

    def pass_core(x, m):
        ref = chunk_of(x, m)
        copy("a4", x * n + m, x * n + m, ref, ref, core_row, rep).start()

    def a1_arrival(m):
        ref = chunk_of(xl, m)
        arrived("a1", m, chunk)
        copy("a3", m, m, ref, ref, lo_row, rep).start()
        pass_core(xl, m)

    loop(0, n, a1_arrival)

    def d3_step(o):
        i = lax.rem(z + o, half)
        m = xl * half + i
        arrived("d1", m, d1r.at[m])
        arrived("d2", i, d2r.at[i])
        total = pb[c * n + m].astype(F32) + d1r[m].astype(F32) + d2r[i].astype(F32)
        d3s[i] = total.astype(BF)
        for k in range(2):
            r, q = owner(k, i)
            send_or_keep("d3", k * half + i, z, d3s.at[i, k], d3r.at[z], r, q)

    loop(0, half, d3_step)

    def a3_arrival(m):
        arrived("a3", m, chunk)
        pass_core(1 - xl, m)

    loop(0, n, a3_arrival)
    ins[4].wait()
    ins[5].wait()
    weff[...] = jnp.where(wm[...] != 0, w[...].astype(F32), 0.0).astype(BF)
    loop(0, 2 * n, lambda m: arrived("a4", m, chunk))

    for t in range(tiles):
        _, _, kt, jt = picks[t]
        rsf[t] = pj[pl.ds(jt * cpt, cpt), kt].reshape(side, width)
    rs[...] = (
        jnp.dot(rsf[...].reshape(tiles * side, width), weff[...], preferred_element_type=F32)
        .astype(BF)
        .reshape(tiles, side, width)
    )

    chunks_pair = 2 * side // chunk_rows
    pairs_half = block // 2 // (2 * side)

    def forward_pair(u):
        for h in range(2):
            for t in range(tiles):
                live, it, _, _ = picks[t]
                cond = jnp.logical_and(live, it == 2 * u + h)
                lhs[h * side:(h + 1) * side, t * side:(t + 1) * side] = chosen(cond, mk[t])
        total = jnp.dot(lhs[...], rs[...].reshape(tiles * side, width), preferred_element_type=F32)
        yb[pl.ds(u * chunks_pair, chunks_pair), 0:chunk_rows] = total.astype(BF).reshape(
            chunks_pair, chunk_rows, width
        )

    wl[...] = jnp.zeros_like(wl)
    deep = max(1, 256 // (2 * chunk_rows))

    def weight_step(i):
        at = pl.ds(i * deep, deep)
        left_side = pj[at].reshape(2 * deep * chunk_rows, width)
        right_side = pb[at].reshape(2 * deep * chunk_rows, width)
        wl[...] += lax.dot_general(
            left_side, right_side, (((0,), (0,)), ((), ())), preferred_element_type=F32
        )

    loop(0, reps // deep, weight_step)
    yb[:, chunk_rows:] = wl[...].astype(BF).reshape(reps, width // reps, width)

    loop(0, pairs_half, lambda i: forward_pair((1 - xh) * pairs_half + i))

    def c1_step(o):
        yy = around(y, o)
        copy("c1", yy, yy, yb.at[(1 - xh) * n + yy], c1r.at[yy], row, hi_rep).start()

    loop(1, n + 1, c1_step)

    loop(0, pairs_half, lambda i: forward_pair(xh * pairs_half + i))

    def pass_hi(name, ref, yy):
        at = xh * n + yy
        copy(name, yy, yy, ref.at[at], ref.at[at], row, hi_rep).start()

    def pass_y(name, ref, o):
        yy = around(y, o)
        copy(name, yy, y, ref.at[rep], ref.at[rep], row, xh * n + yy).start()

    loop(0, n, lambda i: arrived("d3", i, chunk))
    gc[rep] = functools.reduce(jnp.add, [d3r[i].astype(F32) for i in range(n)]).astype(BF)
    pass_hi("d6", gc, y)
    loop(1, n, lambda o: pass_y("d5", gc, o))

    def c2_sum(yy):
        arrived("c1", yy, c1r.at[yy])
        return yb[xh * n + yy].astype(F32) + c1r[yy].astype(F32)

    def c2_step(o):
        yy = around(y, o)
        c2s[yy] = c2_sum(yy).astype(BF)
        copy("c2", yy, y, c2s.at[yy], c2r.at[y], row, xh * n + yy).start()

    loop(1, n, c2_step)
    c2o[...] = c2_sum(y)

    def relay(got, gone, ref, o):
        yy = around(y, o)
        arrived(got, yy, ref.at[rep])
        pass_hi(gone, ref, yy)

    loop(1, n, lambda o: relay("d5", "d6", gc, o))

    def c2_add(o):
        yy = around(y, o)
        arrived("c2", yy, c2r.at[yy])
        c2o[...] += c2r[yy].astype(F32)

    loop(1, n, c2_add)

    def edge_tile(t):
        scores = lax.dot_general(gs[t], rs[t], (((1,), (1,)), ((), ())), preferred_element_type=F32)
        ge[t] = chosen(picks[t][0], tv[t].astype(F32) * scores)

    partners = [core_row, lo_row]
    for bit in range(doublings(n)):
        up = 1 - 2 * lax.rem(z // 2**bit, 2)
        partners.append(row_of(z + up * 2**bit, xl, c))

    def w5_send(i):
        copy("w5", i, i, w5s.at[i], w5r.at[i], partners[i], rep).start()

    def w5_step(i):
        arrived("w5", i, w5r.at[i])
        w5s[i + 1] = w5s[i] + w5r[i]

    w5s[0] = c2o[chunk_rows:]
    w5_send(0)
    oc[rep, 0:chunk_rows] = c2o[0:chunk_rows].astype(BF)
    w5_step(0)
    w5_send(1)
    for t in range(tiles // 2):
        edge_tile(t)
    w5_step(1)
    w5_send(2)
    for t in range(tiles // 2, tiles):
        edge_tile(t)
    outs = [pltpu.make_async_copy(ge, ge_h, local.at[0])]
    outs[-1].start()
    w5_step(2)
    for i in range(3, len(partners)):
        w5_send(i)
        w5_step(i)
    oc[rep, chunk_rows:] = w5s[len(partners)].astype(BF)
    pass_hi("c4", oc, y)
    loop(1, n, lambda o: pass_y("c3", oc, o))

    loop(0, n, lambda yy: arrived("d6", yy, chunk))
    fg[...] = lax.dot_general(
        gc[...].reshape(block, width), weff[...], (((1,), (1,)), ((), ())), preferred_element_type=F32
    ).astype(BF)
    outs.append(pltpu.make_async_copy(fg, fg_h, local.at[1]))
    outs[-1].start()

    loop(1, n, lambda o: relay("c3", "c4", oc, o))
    loop(0, n, lambda yy: arrived("c4", yy, oc.at[rep]))
    outs.append(pltpu.make_async_copy(oc.at[:, pl.ds(0, chunk_rows)], out_h, local.at[2]))
    outs[-1].start()
    total = oc[:, chunk_rows:].astype(F32).reshape(width, width)
    wgo[...] = jnp.where(wm[...] != 0, total, 0.0)
    outs.append(pltpu.make_async_copy(wgo, wg_h, local.at[3]))
    outs[-1].start()

    def left_if_sent(name, i, r, q):
        pl.when(jnp.logical_not(is_me(r, q)))(functools.partial(left, name, i, chunk))

    loop(0, n, lambda i: left_if_sent("a1", i, *reader(i)))
    loop(0, n, lambda m: left_if_sent("d3", m, *owner(m // half, lax.rem(m, half))))

    def along(o):
        yy = around(y, o)
        left("d5", yy, chunk)
        left("c2", yy, c2s.at[yy])
        left("c3", yy, oc.at[rep])

    def across(i):
        left("a3", i, chunk)
        left("d1", i, d1r.at[0])
        left("d6", i, chunk)
        left("c1", i, c1r.at[i])
        left("c4", i, oc.at[rep])
        left("a4", i, chunk)
        left("a4", n + i, chunk)

    loop(1, n, along)
    loop(0, n, across)
    loop(0, half, lambda i: left("d2", i, d1r.at[0]))
    for i in range(len(partners)):
        left("w5", i, w5s.at[i])
    for out in outs:
        out.wait()


def settle_kernel(*refs):
    ins, outs, held = refs[:4], refs[4:8], refs[8:12]
    sem = refs[12]
    loads = [pltpu.make_async_copy(ins[i], held[i], sem.at[i]) for i in range(4)]
    stores = [pltpu.make_async_copy(held[i], outs[i], sem.at[4 + i]) for i in range(4)]
    for one in loads:
        one.start()
    for load, store in zip(loads, stores):
        load.wait()
        store.start()
    for one in stores:
        one.wait()


def settle(*arrays):
    anywhere = pl.BlockSpec(memory_space=pl.ANY)
    return pl.pallas_call(
        settle_kernel,
        out_shape=tuple(jax.ShapeDtypeStruct(a.shape, a.dtype) for a in arrays),
        in_specs=[anywhere] * 4,
        out_specs=(anywhere,) * 4,
        scratch_shapes=[pltpu.VMEM(a.shape, a.dtype) for a in arrays]
        + [pltpu.SemaphoreType.DMA((8,))],
        compiler_params=pltpu.CompilerParams(vmem_limit_bytes=VMEM_MIB * 1024 * 1024),
        name="settle",
    )(*arrays)


def on_device(feats, weight, weight_mask, tile_vals, edge_mask, tile_pos, grad_out):
    reps = lax.axis_size("rep")
    n = reps // 2
    block, width = feats.shape
    tiles, side, _ = tile_vals.shape
    rows = block // reps
    share = width // reps
    steps = 2 + doublings(n)
    places, total = semaphore_places(n)
    chunked = (reps, rows, width)
    pair = (2, rows, width)
    wider = (rows + share, width)

    def vm(shape, kind=BF):
        return pltpu.VMEM(shape, kind)

    scratch = [
        vm(chunked[1:]), vm((block // side, side, width)), vm((width, width)), vm((width, width), jnp.int32),
        vm((tiles, side, side)), vm((tiles, side, side), F32),
        vm((width, width)), vm((reps,) + pair),
        vm((tiles, side, side)), vm((tiles, side, side)),
        vm((tiles, side, width)), vm((tiles, side, width)), vm((tiles, side, width)),
        vm((2 * side, tiles * side)), vm((reps,) + pair),
        vm((n,) + pair), vm((n // 2,) + pair), vm((n // 2,) + pair), vm((n // 2,) + pair),
        vm((n,) + chunked[1:]), vm(chunked),
        vm((reps,) + wider), vm((n,) + wider), vm((n,) + wider), vm((n,) + wider),
        vm(wider, F32), vm((reps,) + wider),
        vm((width, width), F32), vm((steps + 1, share, width), F32), vm((steps, share, width), F32),
        vm((width, width), F32),
        vm((tiles, side, side), F32), vm((block, width)),
        pltpu.SemaphoreType.DMA((total,)), pltpu.SemaphoreType.DMA((total,)),
        pltpu.SemaphoreType.DMA((6,)),
        pltpu.SemaphoreType.REGULAR, pltpu.SemaphoreType.REGULAR,
    ]
    anywhere = pl.BlockSpec(memory_space=pl.ANY)
    out, fgrad, wgrad, edge = pl.pallas_call(
        functools.partial(kernel, n, places),
        out_shape=(
            jax.ShapeDtypeStruct(chunked, BF),
            jax.ShapeDtypeStruct((block, width), BF),
            jax.ShapeDtypeStruct((width, width), F32),
            jax.ShapeDtypeStruct((tiles, side, side), F32),
        ),
        in_specs=[pl.BlockSpec(memory_space=pltpu.SMEM)] + [anywhere] * 6,
        out_specs=(anywhere,) * 4,
        scratch_shapes=scratch,
        compiler_params=pltpu.CompilerParams(
            collective_id=0, has_side_effects=True, vmem_limit_bytes=VMEM_MIB * 1024 * 1024
        ),
        cost_estimate=pl.CostEstimate(
            flops=3_000_000_000, bytes_accessed=5_000_000, transcendentals=0
        ),
        name="layer",
    )(
        tile_pos,
        feats.reshape(chunked),
        grad_out.reshape(block // side, side, width),
        weight,
        weight_mask,
        tile_vals,
        edge_mask,
    )
    return settle(out.reshape(block, width), fgrad, wgrad, edge)


def solution(mesh):
    placed = (
        P("row", None),
        P(),
        P(),
        P(("row", "rep"), None, None),
        P(("row", "rep"), None, None),
        P(("row", "rep")),
        P("row", None),
    )
    return jax.shard_map(
        on_device,
        mesh=mesh,
        in_specs=placed,
        out_specs=(P("row", None), P("row", None), P(), P(("row", "rep"), None, None)),
        check_vma=False,
    )
```

```python
import functools

import jax
import jax.numpy as jnp
from jax import lax
from jax.experimental import pallas as pl
from jax.experimental.pallas import tpu as pltpu
from jax.sharding import PartitionSpec as P

BF = jnp.bfloat16
F32 = jnp.float32
VMEM_MIB = 56


def semaphore_places(n):
    counts = dict(
        a1=2, a2=n, a3=n, a4=2 * n,
        d1=2 * n, d2=n, d3=n, d4=2, d5=n, d6=n,
        c1=n, c2=n, c3=n, c4=n,
        wz=n, wc=4, wy=n, wx=n,
    )
    places, total = {}, 0
    for name, count in counts.items():
        places[name] = total
        total += count
    return places, total


def loop(low, high, step):
    def run(i, carry):
        step(i)
        return carry

    lax.fori_loop(low, high, run, 0)


def kernel(
    n, places,
    pos_ref, feats_h, gout_h, w_h, wm_h, tv_h, em_h,
    out_h, fg_h, wg_h, ge_h,
    chunk, gout, w, wm, tv, em,
    weff, pj, mk, mkt, gs, rsf, rs, lhs, pb,
    d1r, d2s, d2r, d3s, d3r, d3o, d4s, gc,
    yb, c1r, c2s, c2r, c2o, oc,
    wl, wz, wc, wa, wgo, ge, fg,
    send, recv, local,
):
    row, rep = lax.axis_index("row"), lax.axis_index("rep")
    z, xl, c = row // 4, row // 2 % 2, row % 2
    xh, y = rep // n, rep % n
    reps = 2 * n
    tiles, side, _ = tv.shape
    width = w.shape[0]
    piece_rows = pj.shape[2]
    per_side = gout.shape[0]
    ppt = side // piece_rows
    block = per_side * side

    def row_of(zz, xx, cc):
        return zz * 4 + xx * 2 + cc

    core_row, lo_row, both_row = row_of(z, xl, 1 - c), row_of(z, 1 - xl, c), row_of(z, 1 - xl, 1 - c)
    hi_rep = (1 - xh) * n + y
    mine = (c * 2 + xl) * n + z

    def around(at, o):
        return lax.rem(at + o, n)

    def copy(name, i, j, src, dst, to_row, to_rep):
        return pltpu.make_async_remote_copy(
            src_ref=src,
            dst_ref=dst,
            send_sem=send.at[places[name] + i],
            recv_sem=recv.at[places[name] + j],
            device_id=(to_row, to_rep),
            device_id_type=pl.DeviceIdType.MESH,
        )

    def arrived(name, j, ref):
        copy(name, 0, j, ref, ref, core_row, rep).wait_recv()

    def left(name, i, ref):
        copy(name, i, 0, ref, ref, core_row, rep).wait_send()

    owner_rows, owner_rep = [k * reps + rep for k in range(2)], mine // 2
    own_half = lax.rem(mine, 2)
    section, group = row // reps, lax.rem(row, reps)
    part_rows, parts = [], []
    for e in range(2):
        p = 2 * rep + e
        parts.append(p)
        part_rows.append(row_of(lax.rem(p, n), lax.rem(p // n, 2), p // (2 * n)))

    def is_me(r, q):
        return jnp.logical_and(r == row, q == rep)

    ins = []
    for i, (src, dst) in enumerate(
        ((feats_h.at[rep], chunk), (tv_h, tv), (em_h, em), (gout_h, gout), (w_h, w), (wm_h, wm))
    ):
        ins.append(pltpu.make_async_copy(src, dst, local.at[i]))
        ins[-1].start()

    barrier = pltpu.get_barrier_semaphore()

    def greet(r, q):
        pl.semaphore_signal(barrier, inc=1, device_id=(r, q), device_id_type=pl.DeviceIdType.MESH)

    greet(core_row, rep)
    greet(lo_row, rep)
    greet(both_row, rep)
    greet(row, hi_rep)
    loop(1, n, lambda o: greet(row_of(around(z, o), xl, c), rep))
    loop(1, n, lambda o: greet(row, xh * n + around(y, o)))
    expected = 4 + 2 * (n - 1)
    for k in range(2):
        for r, q in ((owner_rows[k], owner_rep), (part_rows[k], group)):
            other = jnp.logical_not(is_me(r, q))
            pl.when(other)(functools.partial(greet, r, q))
            expected = expected + other.astype(jnp.int32)

    ins[0].wait()
    pl.semaphore_wait(barrier, expected)

    def scatter_piece(e):
        src, dst = chunk.at[e], pj.at[parts[e], section]
        same = is_me(part_rows[e], group)

        @pl.when(jnp.logical_not(same))
        def _():
            copy("a1", e, section, src, dst, part_rows[e], group).start()

        @pl.when(same)
        def _():
            pltpu.make_async_copy(src, dst, recv.at[places["a1"] + section]).start()

    scatter_piece(0)
    scatter_piece(1)

    picks = []
    for t in range(tiles):
        pos = pos_ref[t]
        slot = jnp.maximum(pos, 0)
        picks.append(
            (
                pos >= 0,
                lax.rem(slot // per_side, per_side),
                slot // (per_side * per_side),
                lax.rem(slot, per_side),
            )
        )

    ins[1].wait()
    ins[2].wait()
    ins[3].wait()
    for t in range(tiles):
        product = tv[t].astype(F32) * em[t]
        mk[t] = product.astype(BF)
        mkt[t] = product.T.astype(BF)
        gs[t] = gout[picks[t][1]]

    def chosen(cond, tile):
        return lax.select_n(cond, jnp.zeros_like(tile), tile)

    def backward_tile(jj):
        for k in range(2):
            for t in range(tiles):
                live, _, kt, jt = picks[t]
                cond = jnp.logical_and(live, jnp.logical_and(kt == k, jt == jj))
                lhs[k * side:(k + 1) * side, t * side:(t + 1) * side] = chosen(cond, mkt[t])
        total = jnp.dot(lhs[...], gs[...].reshape(tiles * side, width), preferred_element_type=F32)
        total = total.astype(BF)
        for k in range(2):
            pb[pl.ds(jj * ppt, ppt), k] = total[k * side:(k + 1) * side].reshape(ppt, piece_rows, width)

    quarter_tiles = n // ppt

    def send_quarter(x):
        def one(i):
            m = x * n + i
            copy("d1", m, m, pb.at[(1 - c) * 2 * n + m], d1r.at[m], core_row, rep).start()

        first = ((1 - c) * 2 + x) * quarter_tiles
        loop(0, quarter_tiles, lambda i: backward_tile(first + i))
        loop(0, n, one)

    send_quarter(1 - xl)
    send_quarter(xl)

    arrived("a1", 0, chunk.at[0])
    arrived("a1", 1, chunk.at[0])

    def pass_lo(zz):
        p = (c * 2 + xl) * n + zz
        copy("a3", zz, zz, pj.at[p], pj.at[p], lo_row, rep).start()

    def pass_core(m):
        p = c * 2 * n + m
        copy("a4", m, m, pj.at[p], pj.at[p], core_row, rep).start()

    def pass_z(o):
        zz = around(z, o)
        copy("a2", zz, z, pj.at[mine], pj.at[mine], row_of(zz, xl, c), rep).start()

    pass_lo(z)
    loop(1, n, pass_z)
    pass_core(xl * n + z)

    loop(0, 2 * quarter_tiles, lambda i: backward_tile(c * 2 * quarter_tiles + i))

    def d2_step(o):
        zz = around(z, o)
        m = (1 - xl) * n + zz
        arrived("d1", m, d1r.at[m])
        d2s[zz] = (pb[c * 2 * n + m].astype(F32) + d1r[m].astype(F32)).astype(BF)
        copy("d2", zz, zz, d2s.at[zz], d2r.at[zz], lo_row, rep).start()

    loop(1, n + 1, d2_step)

    def a2_step(o):
        zz = around(z, o)
        arrived("a2", zz, a2_like)
        pass_lo(zz)
        pass_core(xl * n + zz)

    a2_like = pj.at[mine]
    loop(1, n, a2_step)

    def d3_sum(zz):
        m = xl * n + zz
        arrived("d1", m, d1r.at[m])
        arrived("d2", zz, d2r.at[zz])
        return pb[c * 2 * n + m].astype(F32) + d1r[m].astype(F32) + d2r[zz].astype(F32)

    def d3_step(o):
        zz = around(z, o)
        d3s[zz] = d3_sum(zz).astype(BF)
        copy("d3", zz, z, d3s.at[zz], d3r.at[z], row_of(zz, xl, c), rep).start()

    loop(1, n, d3_step)
    d3o[...] = d3_sum(z)

    def a3_step(o):
        zz = around(z, o)
        arrived("a3", zz, a2_like)
        pass_core((1 - xl) * n + zz)

    loop(0, n, a3_step)

    def d3_add(o):
        zz = around(z, o)
        arrived("d3", zz, d3r.at[zz])
        d3o[...] += d3r[zz].astype(F32)

    loop(1, n, d3_add)
    d4s[...] = d3o[...].astype(BF)
    for k in range(2):
        same = is_me(owner_rows[k], owner_rep)
        src, dst = d4s.at[k], gc.at[owner_rep, own_half]

        @pl.when(jnp.logical_not(same))
        def _(src=src, dst=dst, k=k):
            copy("d4", k, own_half, src, dst, owner_rows[k], owner_rep).start()

        @pl.when(same)
        def _(src=src, dst=dst):
            pltpu.make_async_copy(src, dst, recv.at[places["d4"] + own_half]).start()

    ins[4].wait()
    ins[5].wait()
    weff[...] = jnp.where(wm[...] != 0, w[...].astype(F32), 0.0).astype(BF)
    loop(0, 2 * n, lambda m: arrived("a4", m, a2_like))

    chunk_rows = 2 * piece_rows
    wl[...] = jnp.zeros_like(wl)
    deep = 2 * side // chunk_rows

    def weight_step(i):
        at = pl.ds(i * deep, deep)
        left_side = pj[at].reshape(deep * chunk_rows, width)
        right_side = pb[at].reshape(deep * chunk_rows, width)
        wl[...] += lax.dot_general(
            left_side, right_side, (((0,), (0,)), ((), ())), preferred_element_type=F32
        )

    loop(0, 4 * n // deep, weight_step)
    yb[:, chunk_rows:] = wl[...].astype(BF).reshape(reps, width // reps, width)

    for t in range(tiles):
        _, _, kt, jt = picks[t]
        rsf[t] = pj[pl.ds(jt * ppt, ppt), kt].reshape(side, width)
    rs[...] = (
        jnp.dot(rsf[...].reshape(tiles * side, width), weff[...], preferred_element_type=F32)
        .astype(BF)
        .reshape(tiles, side, width)
    )

    chunks_pair = 2 * side // (2 * piece_rows)
    pairs_half = block // 2 // (2 * side)

    def forward_pair(u):
        for h in range(2):
            for t in range(tiles):
                live, it, _, _ = picks[t]
                cond = jnp.logical_and(live, it == 2 * u + h)
                lhs[h * side:(h + 1) * side, t * side:(t + 1) * side] = chosen(cond, mk[t])
        total = jnp.dot(lhs[...], rs[...].reshape(tiles * side, width), preferred_element_type=F32)
        yb[pl.ds(u * chunks_pair, chunks_pair), 0:chunk_rows] = total.astype(BF).reshape(
            chunks_pair, 2 * piece_rows, width
        )

    loop(0, pairs_half, lambda i: forward_pair((1 - xh) * pairs_half + i))

    def c1_step(o):
        yy = around(y, o)
        copy("c1", yy, yy, yb.at[(1 - xh) * n + yy], c1r.at[yy], row, hi_rep).start()

    loop(1, n + 1, c1_step)
    loop(0, pairs_half, lambda i: forward_pair(xh * pairs_half + i))

    def pass_hi(name, ref, yy):
        at = xh * n + yy
        copy(name, yy, yy, ref.at[at], ref.at[at], row, hi_rep).start()

    def pass_y(name, ref, o):
        yy = around(y, o)
        copy(name, yy, y, ref.at[rep], ref.at[rep], row, xh * n + yy).start()

    arrived("d4", 0, d4s.at[0])
    arrived("d4", 1, d4s.at[0])
    pass_hi("d6", gc, y)
    loop(1, n, lambda o: pass_y("d5", gc, o))

    def c2_sum(yy):
        arrived("c1", yy, c1r.at[yy])
        return yb[xh * n + yy].astype(F32) + c1r[yy].astype(F32)

    def c2_step(o):
        yy = around(y, o)
        c2s[yy] = c2_sum(yy).astype(BF)
        copy("c2", yy, y, c2s.at[yy], c2r.at[y], row, xh * n + yy).start()

    loop(1, n, c2_step)
    c2o[...] = c2_sum(y)

    def relay(got, gone, ref, o):
        yy = around(y, o)
        arrived(got, yy, ref.at[rep])
        pass_hi(gone, ref, yy)

    loop(1, n, lambda o: relay("d5", "d6", gc, o))

    def c2_add(o):
        yy = around(y, o)
        arrived("c2", yy, c2r.at[yy])
        c2o[...] += c2r[yy].astype(F32)

    loop(1, n, c2_add)

    wz[z] = c2o[chunk_rows:]

    def wz_step(o):
        zz = around(z, o)
        copy("wz", zz, z, wz.at[z], wz.at[z], row_of(zz, xl, c), rep).start()

    loop(1, n, wz_step)
    oc[rep] = c2o[0:chunk_rows].astype(BF)
    pass_hi("c4", oc, y)
    loop(1, n, lambda o: pass_y("c3", oc, o))

    def edge_tile(t):
        scores = lax.dot_general(gs[t], rs[t], (((1,), (1,)), ((), ())), preferred_element_type=F32)
        ge[t] = chosen(picks[t][0], tv[t].astype(F32) * scores)

    for t in range(tiles // 2):
        edge_tile(t)

    loop(1, n, lambda o: arrived("wz", around(z, o), wz.at[z]))
    spot = xl * 2 + c
    wc[spot] = functools.reduce(jnp.add, [wz[i] for i in range(n)])
    for r, s in (
        (core_row, xl * 2 + 1 - c), (lo_row, (1 - xl) * 2 + c), (both_row, (1 - xl) * 2 + 1 - c)
    ):
        copy("wc", s, spot, wc.at[spot], wc.at[spot], r, rep).start()

    for t in range(tiles // 2, tiles):
        edge_tile(t)
    outs = [pltpu.make_async_copy(ge, ge_h, local.at[0])]
    outs[-1].start()

    for i in range(1, 4):
        arrived("wc", lax.rem(spot + i, 4), wc.at[spot])
    wa[rep] = (wc[0] + wc[1]) + (wc[2] + wc[3])
    pass_hi("wx", wa, y)
    loop(1, n, lambda o: pass_y("wy", wa, o))

    loop(1, n, lambda o: relay("c3", "c4", oc, o))

    loop(0, n, lambda yy: arrived("d6", yy, gc.at[rep]))
    fg[...] = lax.dot_general(
        gc[...].reshape(block, width), weff[...], (((1,), (1,)), ((), ())), preferred_element_type=F32
    ).astype(BF)
    outs.append(pltpu.make_async_copy(fg, fg_h, local.at[1]))
    outs[-1].start()

    loop(1, n, lambda o: relay("wy", "wx", wa, o))
    loop(0, n, lambda yy: arrived("c4", yy, oc.at[rep]))
    outs.append(pltpu.make_async_copy(oc, out_h, local.at[2]))
    outs[-1].start()
    loop(0, n, lambda yy: arrived("wx", yy, wa.at[rep]))
    wgo[...] = jnp.where(wm[...] != 0, wa[...].reshape(width, width), 0.0)
    outs.append(pltpu.make_async_copy(wgo, wg_h, local.at[3]))
    outs[-1].start()

    for k in range(2):
        pl.when(jnp.logical_not(is_me(part_rows[k], group)))(functools.partial(left, "a1", k, chunk.at[0]))
        pl.when(jnp.logical_not(is_me(owner_rows[k], owner_rep)))(
            functools.partial(left, "d4", k, d4s.at[0])
        )

    def along_z(o):
        zz = around(z, o)
        left("a2", zz, a2_like)
        left("d3", zz, a2_like)
        left("wz", zz, wz.at[z])

    def along_y(o):
        yy = around(y, o)
        left("d5", yy, gc.at[rep])
        left("c2", yy, c2s.at[yy])
        left("c3", yy, oc.at[rep])
        left("wy", yy, wa.at[rep])

    def across(i):
        left("a3", i, a2_like)
        left("d2", i, a2_like)
        left("d6", i, gc.at[rep])
        left("c1", i, c1r.at[i])
        left("c4", i, oc.at[rep])
        left("wx", i, wa.at[rep])

    def cores(m):
        left("a4", m, a2_like)
        left("d1", m, a2_like)

    loop(1, n, along_z)
    loop(1, n, along_y)
    loop(0, n, across)
    loop(0, 2 * n, cores)
    for i in range(1, 4):
        left("wc", lax.rem(spot + i, 4), wc.at[spot])
    for out in outs:
        out.wait()


def settle_kernel(*refs):
    ins, outs, held = refs[:4], refs[4:8], refs[8:12]
    sem = refs[12]
    loads = [pltpu.make_async_copy(ins[i], held[i], sem.at[i]) for i in range(4)]
    stores = [pltpu.make_async_copy(held[i], outs[i], sem.at[4 + i]) for i in range(4)]
    for one in loads:
        one.start()
    for load, store in zip(loads, stores):
        load.wait()
        store.start()
    for one in stores:
        one.wait()


def settle(*arrays):
    anywhere = pl.BlockSpec(memory_space=pl.ANY)
    return pl.pallas_call(
        settle_kernel,
        out_shape=tuple(jax.ShapeDtypeStruct(a.shape, a.dtype) for a in arrays),
        in_specs=[anywhere] * 4,
        out_specs=(anywhere,) * 4,
        scratch_shapes=[pltpu.VMEM(a.shape, a.dtype) for a in arrays]
        + [pltpu.SemaphoreType.DMA((8,))],
        compiler_params=pltpu.CompilerParams(vmem_limit_bytes=VMEM_MIB * 1024 * 1024),
        name="settle",
    )(*arrays)


def on_device(feats, weight, weight_mask, tile_vals, edge_mask, tile_pos, grad_out):
    reps = lax.axis_size("rep")
    n = reps // 2
    block, width = feats.shape
    tiles, side, _ = tile_vals.shape
    rows = block // (4 * n)
    share = width // reps
    places, total = semaphore_places(n)
    chunked = (reps, 2 * rows, width)
    piece = (2, rows, width)
    wider = (2 * rows + share, width)

    def vm(shape, kind=BF):
        return pltpu.VMEM(shape, kind)

    scratch = [
        vm(piece), vm((block // side, side, width)), vm((width, width)), vm((width, width), jnp.int32),
        vm((tiles, side, side)), vm((tiles, side, side), F32),
        vm((width, width)), vm((4 * n,) + piece),
        vm((tiles, side, side)), vm((tiles, side, side)),
        vm((tiles, side, width)), vm((tiles, side, width)), vm((tiles, side, width)),
        vm((2 * side, tiles * side)), vm((4 * n,) + piece),
        vm((2 * n,) + piece), vm((n,) + piece), vm((n,) + piece), vm((n,) + piece), vm((n,) + piece),
        vm(piece, F32), vm(piece), vm((reps,) + piece),
        vm((reps,) + wider), vm((n,) + wider), vm((n,) + wider), vm((n,) + wider),
        vm(wider, F32), vm(chunked),
        vm((width, width), F32), vm((n, share, width), F32),
        vm((4, share, width), F32), vm((reps, share, width), F32), vm((width, width), F32),
        vm((tiles, side, side), F32), vm((block, width)),
        pltpu.SemaphoreType.DMA((total,)), pltpu.SemaphoreType.DMA((total,)),
        pltpu.SemaphoreType.DMA((6,)),
    ]
    anywhere = pl.BlockSpec(memory_space=pl.ANY)
    out, fgrad, wgrad, edge = pl.pallas_call(
        functools.partial(kernel, n, places),
        out_shape=(
            jax.ShapeDtypeStruct(chunked, BF),
            jax.ShapeDtypeStruct((block, width), BF),
            jax.ShapeDtypeStruct((width, width), F32),
            jax.ShapeDtypeStruct((tiles, side, side), F32),
        ),
        in_specs=[pl.BlockSpec(memory_space=pltpu.SMEM)] + [anywhere] * 6,
        out_specs=(anywhere,) * 4,
        scratch_shapes=scratch,
        compiler_params=pltpu.CompilerParams(
            collective_id=0, has_side_effects=True, vmem_limit_bytes=VMEM_MIB * 1024 * 1024
        ),
        cost_estimate=pl.CostEstimate(
            flops=3_000_000_000, bytes_accessed=5_000_000, transcendentals=0
        ),
        name="layer",
    )(
        tile_pos,
        feats.reshape((reps,) + piece),
        grad_out.reshape(block // side, side, width),
        weight,
        weight_mask,
        tile_vals,
        edge_mask,
    )
    return settle(out.reshape(block, width), fgrad, wgrad, edge)


def solution(mesh):
    placed = (
        P("row", None),
        P(),
        P(),
        P(("row", "rep"), None, None),
        P(("row", "rep"), None, None),
        P(("row", "rep")),
        P("row", None),
    )
    return jax.shard_map(
        on_device,
        mesh=mesh,
        in_specs=placed,
        out_specs=(P("row", None), P("row", None), P(), P(("row", "rep"), None, None)),
        check_vma=False,
    )
```

```python
import functools

import jax
import jax.numpy as jnp
from jax import lax
from jax.experimental import pallas as pl
from jax.experimental.pallas import tpu as pltpu
from jax.sharding import PartitionSpec as P

BF = jnp.bfloat16
F32 = jnp.float32
VMEM_MIB = 56


def semaphore_places(n):
    counts = dict(
        a1=2, a2=n, a3=n, a4=2 * n,
        d1=2 * n, d2=n, d3=n, d4=2, d5=n, d6=n,
        c1=n, c2=n, c3=n, c4=n,
        v1=1, v2=n, wz=n, wc=4, wy=n, wx=n,
    )
    places, total = {}, 0
    for name, count in counts.items():
        places[name] = total
        total += count
    return places, total


def loop(low, high, step):
    def run(i, carry):
        step(i)
        return carry

    lax.fori_loop(low, high, run, 0)


def kernel(
    n, places,
    pos_ref, feats_h, gout_h, w_h, wm_h, tv_h, em_h,
    out_h, fg_h, wg_h, ge_h,
    chunk, gout, w, wm, tv, em,
    weff, pj, mk, mkt, gs, rsf, rs, lhs, pb,
    d1r, d2s, d2r, d3s, d3r, d3o, d4s, gc,
    yb, c1r, c2s, c2r, c2o, oc,
    pbt, lf, wl, wv, v1r, v2s, v2r, wz, wc, wa, wgo, ge, fg,
    send, recv, local,
):
    row, rep = lax.axis_index("row"), lax.axis_index("rep")
    z, xl, c = row // 4, row // 2 % 2, row % 2
    xh, y = rep // n, rep % n
    reps = 2 * n
    tiles, side, _ = tv.shape
    width = w.shape[0]
    piece_rows = pj.shape[2]
    per_side = gout.shape[0]
    ppt = side // piece_rows
    block = per_side * side

    def row_of(zz, xx, cc):
        return zz * 4 + xx * 2 + cc

    core_row, lo_row, both_row = row_of(z, xl, 1 - c), row_of(z, 1 - xl, c), row_of(z, 1 - xl, 1 - c)
    hi_rep = (1 - xh) * n + y
    mine = (c * 2 + xl) * n + z

    def around(at, o):
        return lax.rem(at + o, n)

    def copy(name, i, j, src, dst, to_row, to_rep):
        return pltpu.make_async_remote_copy(
            src_ref=src,
            dst_ref=dst,
            send_sem=send.at[places[name] + i],
            recv_sem=recv.at[places[name] + j],
            device_id=(to_row, to_rep),
            device_id_type=pl.DeviceIdType.MESH,
        )

    def arrived(name, j, ref):
        copy(name, 0, j, ref, ref, core_row, rep).wait_recv()

    def left(name, i, ref):
        copy(name, i, 0, ref, ref, core_row, rep).wait_send()

    owner_rows, owner_rep = [k * reps + rep for k in range(2)], mine // 2
    own_half = lax.rem(mine, 2)
    section, group = row // reps, lax.rem(row, reps)
    part_rows, parts = [], []
    for e in range(2):
        p = 2 * rep + e
        parts.append(p)
        part_rows.append(row_of(lax.rem(p, n), lax.rem(p // n, 2), p // (2 * n)))

    def is_me(r, q):
        return jnp.logical_and(r == row, q == rep)

    ins = []
    for i, (src, dst) in enumerate(
        ((feats_h.at[rep], chunk), (tv_h, tv), (em_h, em), (gout_h, gout), (w_h, w), (wm_h, wm))
    ):
        ins.append(pltpu.make_async_copy(src, dst, local.at[i]))
        ins[-1].start()

    barrier = pltpu.get_barrier_semaphore()

    def greet(r, q):
        pl.semaphore_signal(barrier, inc=1, device_id=(r, q), device_id_type=pl.DeviceIdType.MESH)

    greet(core_row, rep)
    greet(lo_row, rep)
    greet(both_row, rep)
    greet(row, hi_rep)
    loop(1, n, lambda o: greet(row_of(around(z, o), xl, c), rep))
    loop(1, n, lambda o: greet(row, xh * n + around(y, o)))
    expected = 4 + 2 * (n - 1)
    for k in range(2):
        for r, q in ((owner_rows[k], owner_rep), (part_rows[k], group)):
            other = jnp.logical_not(is_me(r, q))
            pl.when(other)(functools.partial(greet, r, q))
            expected = expected + other.astype(jnp.int32)

    ins[0].wait()
    pl.semaphore_wait(barrier, expected)

    def scatter_piece(e):
        src, dst = chunk.at[e], pj.at[parts[e], section]
        same = is_me(part_rows[e], group)

        @pl.when(jnp.logical_not(same))
        def _():
            copy("a1", e, section, src, dst, part_rows[e], group).start()

        @pl.when(same)
        def _():
            pltpu.make_async_copy(src, dst, recv.at[places["a1"] + section]).start()

    scatter_piece(0)
    scatter_piece(1)

    picks = []
    for t in range(tiles):
        pos = pos_ref[t]
        slot = jnp.maximum(pos, 0)
        picks.append(
            (
                pos >= 0,
                lax.rem(slot // per_side, per_side),
                slot // (per_side * per_side),
                lax.rem(slot, per_side),
            )
        )

    ins[1].wait()
    ins[2].wait()
    ins[3].wait()
    for t in range(tiles):
        product = tv[t].astype(F32) * em[t]
        mk[t] = product.astype(BF)
        mkt[t] = product.T.astype(BF)
        gs[t] = gout[picks[t][1]]

    def chosen(cond, tile):
        return lax.select_n(cond, jnp.zeros_like(tile), tile)

    def backward_tile(jj):
        for k in range(2):
            for t in range(tiles):
                live, _, kt, jt = picks[t]
                cond = jnp.logical_and(live, jnp.logical_and(kt == k, jt == jj))
                lhs[k * side:(k + 1) * side, t * side:(t + 1) * side] = chosen(cond, mkt[t])
        total = jnp.dot(lhs[...], gs[...].reshape(tiles * side, width), preferred_element_type=F32)
        total = total.astype(BF)
        for k in range(2):
            pb[pl.ds(jj * ppt, ppt), k] = total[k * side:(k + 1) * side].reshape(ppt, piece_rows, width)

    quarter_tiles = n // ppt

    def send_quarter(x):
        def one(i):
            m = x * n + i
            copy("d1", m, m, pb.at[(1 - c) * 2 * n + m], d1r.at[m], core_row, rep).start()

        first = ((1 - c) * 2 + x) * quarter_tiles
        loop(0, quarter_tiles, lambda i: backward_tile(first + i))
        loop(0, n, one)

    send_quarter(1 - xl)
    send_quarter(xl)

    arrived("a1", 0, chunk.at[0])
    arrived("a1", 1, chunk.at[0])

    def pass_lo(zz):
        p = (c * 2 + xl) * n + zz
        copy("a3", zz, zz, pj.at[p], pj.at[p], lo_row, rep).start()

    def pass_core(m):
        p = c * 2 * n + m
        copy("a4", m, m, pj.at[p], pj.at[p], core_row, rep).start()

    def pass_z(o):
        zz = around(z, o)
        copy("a2", zz, z, pj.at[mine], pj.at[mine], row_of(zz, xl, c), rep).start()

    pass_lo(z)
    loop(1, n, pass_z)
    pass_core(xl * n + z)

    loop(0, 2 * quarter_tiles, lambda i: backward_tile(c * 2 * quarter_tiles + i))

    def d2_step(o):
        zz = around(z, o)
        m = (1 - xl) * n + zz
        arrived("d1", m, d1r.at[m])
        d2s[zz] = (pb[c * 2 * n + m].astype(F32) + d1r[m].astype(F32)).astype(BF)
        copy("d2", zz, zz, d2s.at[zz], d2r.at[zz], lo_row, rep).start()

    loop(1, n + 1, d2_step)

    chunk_rows = 2 * piece_rows
    deep = 2 * side // chunk_rows

    def turn(i):
        rows = pb[pl.ds(i * deep, deep)].reshape(2 * side, width)
        pbt[i] = rows.astype(F32).T.astype(BF)

    loop(0, 4 * n // deep, turn)

    def spread_row(i):
        for t in range(tiles):
            cond = jnp.logical_and(picks[t][0], picks[t][1] == i)
            lf[i, :, t * side:(t + 1) * side] = chosen(cond, mk[t])

    loop(0, per_side, spread_row)

    def a2_step(o):
        zz = around(z, o)
        arrived("a2", zz, a2_like)
        pass_lo(zz)
        pass_core(xl * n + zz)

    a2_like = pj.at[mine]
    loop(1, n, a2_step)

    def a3_step(o):
        zz = around(z, o)
        arrived("a3", zz, a2_like)
        pass_core((1 - xl) * n + zz)

    loop(0, n, a3_step)

    def d3_sum(zz):
        m = xl * n + zz
        arrived("d1", m, d1r.at[m])
        arrived("d2", zz, d2r.at[zz])
        return pb[c * 2 * n + m].astype(F32) + d1r[m].astype(F32) + d2r[zz].astype(F32)

    def d3_step(o):
        zz = around(z, o)
        d3s[zz] = d3_sum(zz).astype(BF)
        copy("d3", zz, z, d3s.at[zz], d3r.at[z], row_of(zz, xl, c), rep).start()

    loop(1, n, d3_step)
    d3o[...] = d3_sum(z)

    ins[4].wait()
    ins[5].wait()
    weff[...] = jnp.where(wm[...] != 0, w[...].astype(F32), 0.0).astype(BF)
    loop(0, 2 * n, lambda m: arrived("a4", m, a2_like))

    wl[...] = jnp.zeros_like(wl)

    def weight_step(i):
        rows = pj[pl.ds(i * deep, deep)].reshape(2 * side, width)
        wl[...] += jnp.dot(pbt[i], rows, preferred_element_type=F32)

    loop(0, 4 * n // deep, weight_step)
    wv[...] = wl[...].T.astype(BF).reshape(wv.shape)
    away = wv.at[pl.ds((1 - xh) * n, n)]
    copy("v1", 0, 0, away, v1r, row, hi_rep).start()

    for t in range(tiles):
        _, _, kt, jt = picks[t]
        rsf[t] = pj[pl.ds(jt * ppt, ppt), kt].reshape(side, width)
    rs[...] = (
        jnp.dot(rsf[...].reshape(tiles * side, width), weff[...], preferred_element_type=F32)
        .astype(BF)
        .reshape(tiles, side, width)
    )

    chunks_pair = 2 * side // (2 * piece_rows)
    pairs_half = block // 2 // (2 * side)

    def forward_pair(u):
        mine_rows = lf[pl.ds(2 * u, 2)].reshape(2 * side, tiles * side)
        total = jnp.dot(mine_rows, rs[...].reshape(tiles * side, width), preferred_element_type=F32)
        yb[pl.ds(u * chunks_pair, chunks_pair)] = total.astype(BF).reshape(
            chunks_pair, 2 * piece_rows, width
        )

    loop(0, pairs_half, lambda i: forward_pair((1 - xh) * pairs_half + i))

    def c1_step(o):
        yy = around(y, o)
        copy("c1", yy, yy, yb.at[(1 - xh) * n + yy], c1r.at[yy], row, hi_rep).start()

    loop(1, n + 1, c1_step)
    loop(0, pairs_half, lambda i: forward_pair(xh * pairs_half + i))

    def d3_add(o):
        zz = around(z, o)
        arrived("d3", zz, d3r.at[zz])
        d3o[...] += d3r[zz].astype(F32)

    loop(1, n, d3_add)
    d4s[...] = d3o[...].astype(BF)
    for k in range(2):
        same = is_me(owner_rows[k], owner_rep)
        src, dst = d4s.at[k], gc.at[owner_rep, own_half]

        @pl.when(jnp.logical_not(same))
        def _(src=src, dst=dst, k=k):
            copy("d4", k, own_half, src, dst, owner_rows[k], owner_rep).start()

        @pl.when(same)
        def _(src=src, dst=dst):
            pltpu.make_async_copy(src, dst, recv.at[places["d4"] + own_half]).start()

    def pass_hi(name, ref, yy):
        at = xh * n + yy
        copy(name, yy, yy, ref.at[at], ref.at[at], row, hi_rep).start()

    def pass_y(name, ref, o):
        yy = around(y, o)
        copy(name, yy, y, ref.at[rep], ref.at[rep], row, xh * n + yy).start()

    copy("v1", 0, 0, away, v1r, row, hi_rep).wait_recv()

    def v2_step(o):
        yy = around(y, o)
        v2s[yy] = (wv[xh * n + yy].astype(F32) + v1r[yy].astype(F32)).astype(BF)
        copy("v2", yy, y, v2s.at[yy], v2r.at[y], row, xh * n + yy).start()

    loop(1, n, v2_step)
    wz[z] = wv[rep].astype(F32) + v1r[y].astype(F32)

    def c2_sum(yy):
        arrived("c1", yy, c1r.at[yy])
        return yb[xh * n + yy].astype(F32) + c1r[yy].astype(F32)

    def c2_step(o):
        yy = around(y, o)
        c2s[yy] = c2_sum(yy).astype(BF)
        copy("c2", yy, y, c2s.at[yy], c2r.at[y], row, xh * n + yy).start()

    loop(1, n, c2_step)
    c2o[...] = c2_sum(y)

    arrived("d4", 0, d4s.at[0])
    arrived("d4", 1, d4s.at[0])
    pass_hi("d6", gc, y)
    loop(1, n, lambda o: pass_y("d5", gc, o))

    def v2_add(o):
        yy = around(y, o)
        arrived("v2", yy, v2r.at[yy])
        wz[z] += v2r[yy].astype(F32)

    loop(1, n, v2_add)

    def wz_step(o):
        zz = around(z, o)
        copy("wz", zz, z, wz.at[z], wz.at[z], row_of(zz, xl, c), rep).start()

    loop(1, n, wz_step)
    def relay(got, gone, ref, o):
        yy = around(y, o)
        arrived(got, yy, ref.at[rep])
        pass_hi(gone, ref, yy)

    loop(1, n, lambda o: relay("d5", "d6", gc, o))

    def c2_add(o):
        yy = around(y, o)
        arrived("c2", yy, c2r.at[yy])
        c2o[...] += c2r[yy].astype(F32)

    loop(1, n, c2_add)

    oc[rep] = c2o[...].astype(BF)
    pass_hi("c4", oc, y)
    loop(1, n, lambda o: pass_y("c3", oc, o))

    def edge_tile(t):
        scores = lax.dot_general(gs[t], rs[t], (((1,), (1,)), ((), ())), preferred_element_type=F32)
        ge[t] = chosen(picks[t][0], tv[t].astype(F32) * scores)

    for t in range(tiles // 2):
        edge_tile(t)

    loop(1, n, lambda o: arrived("wz", around(z, o), wz.at[z]))
    spot = xl * 2 + c
    wc[spot] = functools.reduce(jnp.add, [wz[i] for i in range(n)])
    for r, s in (
        (core_row, xl * 2 + 1 - c), (lo_row, (1 - xl) * 2 + c), (both_row, (1 - xl) * 2 + 1 - c)
    ):
        copy("wc", s, spot, wc.at[spot], wc.at[spot], r, rep).start()

    for t in range(tiles // 2, tiles):
        edge_tile(t)
    outs = [pltpu.make_async_copy(ge, ge_h, local.at[0])]
    outs[-1].start()

    for i in range(1, 4):
        arrived("wc", lax.rem(spot + i, 4), wc.at[spot])
    wa[rep] = (wc[0] + wc[1]) + (wc[2] + wc[3])
    pass_hi("wx", wa, y)
    loop(1, n, lambda o: pass_y("wy", wa, o))

    loop(1, n, lambda o: relay("c3", "c4", oc, o))

    loop(0, n, lambda yy: arrived("d6", yy, gc.at[rep]))
    fg[...] = lax.dot_general(
        gc[...].reshape(block, width), weff[...], (((1,), (1,)), ((), ())), preferred_element_type=F32
    ).astype(BF)
    outs.append(pltpu.make_async_copy(fg, fg_h, local.at[1]))
    outs[-1].start()

    loop(1, n, lambda o: relay("wy", "wx", wa, o))
    loop(0, n, lambda yy: arrived("c4", yy, oc.at[rep]))
    outs.append(pltpu.make_async_copy(oc, out_h, local.at[2]))
    outs[-1].start()
    loop(0, n, lambda yy: arrived("wx", yy, wa.at[rep]))
    wgo[...] = jnp.where(wm[...] != 0, wa[...].reshape(width, width), 0.0)
    outs.append(pltpu.make_async_copy(wgo, wg_h, local.at[3]))
    outs[-1].start()

    for k in range(2):
        pl.when(jnp.logical_not(is_me(part_rows[k], group)))(functools.partial(left, "a1", k, chunk.at[0]))
        pl.when(jnp.logical_not(is_me(owner_rows[k], owner_rep)))(
            functools.partial(left, "d4", k, d4s.at[0])
        )

    def along_z(o):
        zz = around(z, o)
        left("a2", zz, a2_like)
        left("d3", zz, a2_like)
        left("wz", zz, wz.at[z])

    def along_y(o):
        yy = around(y, o)
        left("d5", yy, gc.at[rep])
        left("c2", yy, c2s.at[yy])
        left("v2", yy, v2s.at[yy])
        left("c3", yy, oc.at[rep])
        left("wy", yy, wa.at[rep])

    def across(i):
        left("a3", i, a2_like)
        left("d2", i, a2_like)
        left("d6", i, gc.at[rep])
        left("c1", i, c1r.at[i])
        left("c4", i, oc.at[rep])
        left("wx", i, wa.at[rep])

    def cores(m):
        left("a4", m, a2_like)
        left("d1", m, a2_like)

    loop(1, n, along_z)
    loop(1, n, along_y)
    loop(0, n, across)
    loop(0, 2 * n, cores)
    for i in range(1, 4):
        left("wc", lax.rem(spot + i, 4), wc.at[spot])
    left("v1", 0, v1r)
    for out in outs:
        out.wait()


def settle_kernel(*refs):
    ins, outs, held = refs[:4], refs[4:8], refs[8:12]
    sem = refs[12]
    loads = [pltpu.make_async_copy(ins[i], held[i], sem.at[i]) for i in range(4)]
    stores = [pltpu.make_async_copy(held[i], outs[i], sem.at[4 + i]) for i in range(4)]
    for one in loads:
        one.start()
    for load, store in zip(loads, stores):
        load.wait()
        store.start()
    for one in stores:
        one.wait()


def settle(*arrays):
    anywhere = pl.BlockSpec(memory_space=pl.ANY)
    return pl.pallas_call(
        settle_kernel,
        out_shape=tuple(jax.ShapeDtypeStruct(a.shape, a.dtype) for a in arrays),
        in_specs=[anywhere] * 4,
        out_specs=(anywhere,) * 4,
        scratch_shapes=[pltpu.VMEM(a.shape, a.dtype) for a in arrays]
        + [pltpu.SemaphoreType.DMA((8,))],
        compiler_params=pltpu.CompilerParams(vmem_limit_bytes=VMEM_MIB * 1024 * 1024),
        name="settle",
    )(*arrays)


def on_device(feats, weight, weight_mask, tile_vals, edge_mask, tile_pos, grad_out):
    reps = lax.axis_size("rep")
    n = reps // 2
    block, width = feats.shape
    tiles, side, _ = tile_vals.shape
    rows = block // (4 * n)
    share = width // reps
    places, total = semaphore_places(n)
    chunked = (reps, 2 * rows, width)
    piece = (2, rows, width)
    slices = (share, width)

    def vm(shape, kind=BF):
        return pltpu.VMEM(shape, kind)

    scratch = [
        vm(piece), vm((block // side, side, width)), vm((width, width)), vm((width, width), jnp.int32),
        vm((tiles, side, side)), vm((tiles, side, side), F32),
        vm((width, width)), vm((4 * n,) + piece),
        vm((tiles, side, side)), vm((tiles, side, side)),
        vm((tiles, side, width)), vm((tiles, side, width)), vm((tiles, side, width)),
        vm((2 * side, tiles * side)), vm((4 * n,) + piece),
        vm((2 * n,) + piece), vm((n,) + piece), vm((n,) + piece), vm((n,) + piece), vm((n,) + piece),
        vm(piece, F32), vm(piece), vm((reps,) + piece),
        vm(chunked), vm((n,) + chunked[1:]), vm((n,) + chunked[1:]), vm((n,) + chunked[1:]),
        vm(chunked[1:], F32), vm(chunked),
        vm((2 * block // (2 * side), width, 2 * side)), vm((block // side, side, tiles * side)),
        vm((width, width), F32), vm((reps,) + slices), vm((n,) + slices), vm((n,) + slices), vm((n,) + slices),
        vm((n,) + slices, F32),
        vm((4, share, width), F32), vm((reps, share, width), F32), vm((width, width), F32),
        vm((tiles, side, side), F32), vm((block, width)),
        pltpu.SemaphoreType.DMA((total,)), pltpu.SemaphoreType.DMA((total,)),
        pltpu.SemaphoreType.DMA((6,)),
    ]
    anywhere = pl.BlockSpec(memory_space=pl.ANY)
    out, fgrad, wgrad, edge = pl.pallas_call(
        functools.partial(kernel, n, places),
        out_shape=(
            jax.ShapeDtypeStruct(chunked, BF),
            jax.ShapeDtypeStruct((block, width), BF),
            jax.ShapeDtypeStruct((width, width), F32),
            jax.ShapeDtypeStruct((tiles, side, side), F32),
        ),
        in_specs=[pl.BlockSpec(memory_space=pltpu.SMEM)] + [anywhere] * 6,
        out_specs=(anywhere,) * 4,
        scratch_shapes=scratch,
        compiler_params=pltpu.CompilerParams(
            collective_id=0, has_side_effects=True, vmem_limit_bytes=VMEM_MIB * 1024 * 1024
        ),
        cost_estimate=pl.CostEstimate(
            flops=3_000_000_000, bytes_accessed=5_000_000, transcendentals=0
        ),
        name="layer",
    )(
        tile_pos,
        feats.reshape((reps,) + piece),
        grad_out.reshape(block // side, side, width),
        weight,
        weight_mask,
        tile_vals,
        edge_mask,
    )
    return settle(out.reshape(block, width), fgrad, wgrad, edge)


def solution(mesh):
    placed = (
        P("row", None),
        P(),
        P(),
        P(("row", "rep"), None, None),
        P(("row", "rep"), None, None),
        P(("row", "rep")),
        P("row", None),
    )
    return jax.shard_map(
        on_device,
        mesh=mesh,
        in_specs=placed,
        out_specs=(P("row", None), P("row", None), P(), P(("row", "rep"), None, None)),
        check_vma=False,
    )
```

```python
import functools

import jax
import jax.numpy as jnp
from jax import lax
from jax.experimental import pallas as pl
from jax.experimental.pallas import tpu as pltpu
from jax.sharding import PartitionSpec as P

BF = jnp.bfloat16
F32 = jnp.float32
VMEM_MIB = 56


def semaphore_places(n):
    counts = dict(
        a1=2, a2=n, a3=n, a4=2 * n,
        d1=2 * n, d2=n, d3=n, d4=2, d5=n, d6=n,
        c1=n, c2=n, c3=n, c4=n,
        v1=1, v2=n, wz=n, wc=4, wy=n, wx=n,
    )
    places, total = {}, 0
    for name, count in counts.items():
        places[name] = total
        total += count
    return places, total


def loop(low, high, step):
    def run(i, carry):
        step(i)
        return carry

    lax.fori_loop(low, high, run, 0)


def kernel(
    n, places,
    pos_ref, feats_h, gout_h, w_h, wm_h, tv_h, em_h,
    out_h, fg_h, wg_h, ge_h,
    chunk, gout, w, wm, tv, em,
    weff, pj, mk, mkt, gs, rsf, rs, lhs, pb,
    d1r, d2s, d2r, d3s, d3r, d3o, d4s, gc,
    yb, c1r, c2s, c2r, c2o, oc,
    pbt, lf, wl, wv, v1r, v2s, v2r, wz, wc, wa, wgo, ge, fg,
    send, recv, local,
):
    row, rep = lax.axis_index("row"), lax.axis_index("rep")
    z, xl, c = row // 4, row // 2 % 2, row % 2
    xh, y = rep // n, rep % n
    reps = 2 * n
    tiles, side, _ = tv.shape
    width = w.shape[0]
    piece_rows = pj.shape[2]
    per_side = gout.shape[0]
    ppt = side // piece_rows
    block = per_side * side

    def row_of(zz, xx, cc):
        return zz * 4 + xx * 2 + cc

    core_row, lo_row, both_row = row_of(z, xl, 1 - c), row_of(z, 1 - xl, c), row_of(z, 1 - xl, 1 - c)
    hi_rep = (1 - xh) * n + y
    mine = (c * 2 + xl) * n + z

    def around(at, o):
        return lax.rem(at + o, n)

    def copy(name, i, j, src, dst, to_row, to_rep):
        return pltpu.make_async_remote_copy(
            src_ref=src,
            dst_ref=dst,
            send_sem=send.at[places[name] + i],
            recv_sem=recv.at[places[name] + j],
            device_id=(to_row, to_rep),
            device_id_type=pl.DeviceIdType.MESH,
        )

    def arrived(name, j, ref):
        copy(name, 0, j, ref, ref, core_row, rep).wait_recv()

    def left(name, i, ref):
        copy(name, i, 0, ref, ref, core_row, rep).wait_send()

    owner_rows, owner_rep = [k * reps + rep for k in range(2)], mine // 2
    own_half = lax.rem(mine, 2)
    section, group = row // reps, lax.rem(row, reps)
    part_rows, parts = [], []
    for e in range(2):
        p = 2 * rep + e
        parts.append(p)
        part_rows.append(row_of(lax.rem(p, n), lax.rem(p // n, 2), p // (2 * n)))

    def is_me(r, q):
        return jnp.logical_and(r == row, q == rep)

    ins = []
    for i, (src, dst) in enumerate(
        ((feats_h.at[rep], chunk), (tv_h, tv), (em_h, em), (gout_h, gout), (w_h, w), (wm_h, wm))
    ):
        ins.append(pltpu.make_async_copy(src, dst, local.at[i]))
        ins[-1].start()

    barrier = pltpu.get_barrier_semaphore()

    def greet(r, q):
        pl.semaphore_signal(barrier, inc=1, device_id=(r, q), device_id_type=pl.DeviceIdType.MESH)

    greet(core_row, rep)
    greet(lo_row, rep)
    greet(both_row, rep)
    greet(row, hi_rep)
    loop(1, n, lambda o: greet(row_of(around(z, o), xl, c), rep))
    loop(1, n, lambda o: greet(row, xh * n + around(y, o)))
    expected = 4 + 2 * (n - 1)
    for k in range(2):
        for r, q in ((owner_rows[k], owner_rep), (part_rows[k], group)):
            other = jnp.logical_not(is_me(r, q))
            pl.when(other)(functools.partial(greet, r, q))
            expected = expected + other.astype(jnp.int32)

    ins[0].wait()
    pl.semaphore_wait(barrier, expected)

    def scatter_piece(e):
        src, dst = chunk.at[e], pj.at[parts[e], section]
        same = is_me(part_rows[e], group)

        @pl.when(jnp.logical_not(same))
        def _():
            copy("a1", e, section, src, dst, part_rows[e], group).start()

        @pl.when(same)
        def _():
            pltpu.make_async_copy(src, dst, recv.at[places["a1"] + section]).start()

    scatter_piece(0)
    scatter_piece(1)

    picks = []
    for t in range(tiles):
        pos = pos_ref[t]
        slot = jnp.maximum(pos, 0)
        picks.append(
            (
                pos >= 0,
                lax.rem(slot // per_side, per_side),
                slot // (per_side * per_side),
                lax.rem(slot, per_side),
            )
        )

    ins[1].wait()
    ins[2].wait()
    ins[3].wait()
    for t in range(tiles):
        product = tv[t].astype(F32) * em[t]
        mk[t] = product.astype(BF)
        mkt[t] = product.T.astype(BF)
        gs[t] = gout[picks[t][1]]

    def chosen(cond, tile):
        return lax.select_n(cond, jnp.zeros_like(tile), tile)

    def backward_tile(jj):
        for k in range(2):
            for t in range(tiles):
                live, _, kt, jt = picks[t]
                cond = jnp.logical_and(live, jnp.logical_and(kt == k, jt == jj))
                lhs[k * side:(k + 1) * side, t * side:(t + 1) * side] = chosen(cond, mkt[t])
        total = jnp.dot(lhs[...], gs[...].reshape(tiles * side, width), preferred_element_type=F32)
        total = total.astype(BF)
        for k in range(2):
            pb[pl.ds(jj * ppt, ppt), k] = total[k * side:(k + 1) * side].reshape(ppt, piece_rows, width)

    quarter_tiles = n // ppt

    def send_quarter(x):
        def one(i):
            m = x * n + i
            copy("d1", m, m, pb.at[(1 - c) * 2 * n + m], d1r.at[m], core_row, rep).start()

        first = ((1 - c) * 2 + x) * quarter_tiles
        loop(0, quarter_tiles, lambda i: backward_tile(first + i))
        loop(0, n, one)

    send_quarter(1 - xl)
    send_quarter(xl)

    arrived("a1", 0, chunk.at[0])
    arrived("a1", 1, chunk.at[0])

    def pass_lo(zz):
        p = (c * 2 + xl) * n + zz
        copy("a3", zz, zz, pj.at[p], pj.at[p], lo_row, rep).start()

    def pass_core(m):
        p = c * 2 * n + m
        copy("a4", m, m, pj.at[p], pj.at[p], core_row, rep).start()

    def pass_z(o):
        zz = around(z, o)
        copy("a2", zz, z, pj.at[mine], pj.at[mine], row_of(zz, xl, c), rep).start()

    pass_lo(z)
    loop(1, n, pass_z)
    pass_core(xl * n + z)

    loop(0, 2 * quarter_tiles, lambda i: backward_tile(c * 2 * quarter_tiles + i))

    def d2_step(o):
        zz = around(z, o)
        m = (1 - xl) * n + zz
        arrived("d1", m, d1r.at[m])
        d2s[zz] = (pb[c * 2 * n + m].astype(F32) + d1r[m].astype(F32)).astype(BF)
        copy("d2", zz, zz, d2s.at[zz], d2r.at[zz], lo_row, rep).start()

    loop(1, n + 1, d2_step)

    chunk_rows = 2 * piece_rows
    deep = 2 * side // chunk_rows

    def turn(i):
        rows = pb[pl.ds(i * deep, deep)].reshape(2 * side, width)
        pbt[i] = rows.astype(F32).T.astype(BF)

    loop(0, 4 * n // deep, turn)

    def spread_row(i):
        for t in range(tiles):
            cond = jnp.logical_and(picks[t][0], picks[t][1] == i)
            lf[i, :, t * side:(t + 1) * side] = chosen(cond, mk[t])

    loop(0, per_side, spread_row)

    def a2_step(o):
        zz = around(z, o)
        arrived("a2", zz, a2_like)
        pass_lo(zz)
        pass_core(xl * n + zz)

    a2_like = pj.at[mine]
    loop(1, n, a2_step)

    def d3_sum(zz):
        m = xl * n + zz
        arrived("d1", m, d1r.at[m])
        arrived("d2", zz, d2r.at[zz])
        return pb[c * 2 * n + m].astype(F32) + d1r[m].astype(F32) + d2r[zz].astype(F32)

    def d3_step(o):
        zz = around(z, o)
        d3s[zz] = d3_sum(zz).astype(BF)
        copy("d3", zz, z, d3s.at[zz], d3r.at[z], row_of(zz, xl, c), rep).start()

    loop(1, n, d3_step)
    d3o[...] = d3_sum(z)

    def a3_step(o):
        zz = around(z, o)
        arrived("a3", zz, a2_like)
        pass_core((1 - xl) * n + zz)

    loop(0, n, a3_step)

    ins[4].wait()
    ins[5].wait()
    weff[...] = jnp.where(wm[...] != 0, w[...].astype(F32), 0.0).astype(BF)
    loop(0, 2 * n, lambda m: arrived("a4", m, a2_like))

    wl[...] = jnp.zeros_like(wl)

    def weight_step(i):
        rows = pj[pl.ds(i * deep, deep)].reshape(2 * side, width)
        wl[...] += jnp.dot(pbt[i], rows, preferred_element_type=F32)

    loop(0, 4 * n // deep, weight_step)
    wv[...] = wl[...].T.astype(BF).reshape(wv.shape)
    away = wv.at[pl.ds((1 - xh) * n, n)]
    copy("v1", 0, 0, away, v1r, row, hi_rep).start()

    for t in range(tiles):
        _, _, kt, jt = picks[t]
        rsf[t] = pj[pl.ds(jt * ppt, ppt), kt].reshape(side, width)
    rs[...] = (
        jnp.dot(rsf[...].reshape(tiles * side, width), weff[...], preferred_element_type=F32)
        .astype(BF)
        .reshape(tiles, side, width)
    )

    chunks_pair = 2 * side // (2 * piece_rows)
    pairs_half = block // 2 // (2 * side)

    def forward_pair(u):
        mine_rows = lf[pl.ds(2 * u, 2)].reshape(2 * side, tiles * side)
        total = jnp.dot(mine_rows, rs[...].reshape(tiles * side, width), preferred_element_type=F32)
        yb[pl.ds(u * chunks_pair, chunks_pair)] = total.astype(BF).reshape(
            chunks_pair, 2 * piece_rows, width
        )

    loop(0, pairs_half, lambda i: forward_pair((1 - xh) * pairs_half + i))

    def c1_step(o):
        yy = around(y, o)
        copy("c1", yy, yy, yb.at[(1 - xh) * n + yy], c1r.at[yy], row, hi_rep).start()

    loop(1, n + 1, c1_step)

    def d3_add(o):
        zz = around(z, o)
        arrived("d3", zz, d3r.at[zz])
        d3o[...] += d3r[zz].astype(F32)

    loop(1, n, d3_add)
    d4s[...] = d3o[...].astype(BF)
    for k in range(2):
        same = is_me(owner_rows[k], owner_rep)
        src, dst = d4s.at[k], gc.at[owner_rep, own_half]

        @pl.when(jnp.logical_not(same))
        def _(src=src, dst=dst, k=k):
            copy("d4", k, own_half, src, dst, owner_rows[k], owner_rep).start()

        @pl.when(same)
        def _(src=src, dst=dst):
            pltpu.make_async_copy(src, dst, recv.at[places["d4"] + own_half]).start()

    loop(0, pairs_half, lambda i: forward_pair(xh * pairs_half + i))

    def pass_hi(name, ref, yy):
        at = xh * n + yy
        copy(name, yy, yy, ref.at[at], ref.at[at], row, hi_rep).start()

    def pass_y(name, ref, o):
        yy = around(y, o)
        copy(name, yy, y, ref.at[rep], ref.at[rep], row, xh * n + yy).start()

    copy("v1", 0, 0, away, v1r, row, hi_rep).wait_recv()

    def v2_step(o):
        yy = around(y, o)
        v2s[yy] = (wv[xh * n + yy].astype(F32) + v1r[yy].astype(F32)).astype(BF)
        copy("v2", yy, y, v2s.at[yy], v2r.at[y], row, xh * n + yy).start()

    loop(1, n, v2_step)
    wz[z] = wv[rep].astype(F32) + v1r[y].astype(F32)

    def c2_sum(yy):
        arrived("c1", yy, c1r.at[yy])
        return yb[xh * n + yy].astype(F32) + c1r[yy].astype(F32)

    def c2_step(o):
        yy = around(y, o)
        c2s[yy] = c2_sum(yy).astype(BF)
        copy("c2", yy, y, c2s.at[yy], c2r.at[y], row, xh * n + yy).start()

    loop(1, n, c2_step)
    c2o[...] = c2_sum(y)

    arrived("d4", 0, d4s.at[0])
    arrived("d4", 1, d4s.at[0])
    pass_hi("d6", gc, y)
    loop(1, n, lambda o: pass_y("d5", gc, o))

    def v2_add(o):
        yy = around(y, o)
        arrived("v2", yy, v2r.at[yy])
        wz[z] += v2r[yy].astype(F32)

    loop(1, n, v2_add)

    def wz_step(o):
        zz = around(z, o)
        copy("wz", zz, z, wz.at[z], wz.at[z], row_of(zz, xl, c), rep).start()

    loop(1, n, wz_step)
    def relay(got, gone, ref, o):
        yy = around(y, o)
        arrived(got, yy, ref.at[rep])
        pass_hi(gone, ref, yy)


    def c2_add(o):
        yy = around(y, o)
        arrived("c2", yy, c2r.at[yy])
        c2o[...] += c2r[yy].astype(F32)

    loop(1, n, c2_add)

    oc[rep] = c2o[...].astype(BF)
    pass_hi("c4", oc, y)
    loop(1, n, lambda o: pass_y("c3", oc, o))

    def edge_tile(t):
        scores = lax.dot_general(gs[t], rs[t], (((1,), (1,)), ((), ())), preferred_element_type=F32)
        ge[t] = chosen(picks[t][0], tv[t].astype(F32) * scores)

    for t in range(tiles // 2):
        edge_tile(t)

    loop(1, n, lambda o: arrived("wz", around(z, o), wz.at[z]))
    spot = xl * 2 + c
    wc[spot] = functools.reduce(jnp.add, [wz[i] for i in range(n)])
    for r, s in (
        (core_row, xl * 2 + 1 - c), (lo_row, (1 - xl) * 2 + c), (both_row, (1 - xl) * 2 + 1 - c)
    ):
        copy("wc", s, spot, wc.at[spot], wc.at[spot], r, rep).start()

    loop(1, n, lambda o: relay("d5", "d6", gc, o))

    for t in range(tiles // 2, tiles):
        edge_tile(t)
    outs = [pltpu.make_async_copy(ge, ge_h, local.at[0])]
    outs[-1].start()

    for i in range(1, 4):
        arrived("wc", lax.rem(spot + i, 4), wc.at[spot])
    wa[rep] = (wc[0] + wc[1]) + (wc[2] + wc[3])
    pass_hi("wx", wa, y)
    loop(1, n, lambda o: pass_y("wy", wa, o))

    loop(1, n, lambda o: relay("c3", "c4", oc, o))

    loop(0, n, lambda yy: arrived("d6", yy, gc.at[rep]))
    fg[...] = lax.dot_general(
        gc[...].reshape(block, width), weff[...], (((1,), (1,)), ((), ())), preferred_element_type=F32
    ).astype(BF)
    outs.append(pltpu.make_async_copy(fg, fg_h, local.at[1]))
    outs[-1].start()

    loop(1, n, lambda o: relay("wy", "wx", wa, o))
    loop(0, n, lambda yy: arrived("c4", yy, oc.at[rep]))
    outs.append(pltpu.make_async_copy(oc, out_h, local.at[2]))
    outs[-1].start()
    loop(0, n, lambda yy: arrived("wx", yy, wa.at[rep]))
    wgo[...] = jnp.where(wm[...] != 0, wa[...].reshape(width, width), 0.0)
    outs.append(pltpu.make_async_copy(wgo, wg_h, local.at[3]))
    outs[-1].start()

    for k in range(2):
        pl.when(jnp.logical_not(is_me(part_rows[k], group)))(functools.partial(left, "a1", k, chunk.at[0]))
        pl.when(jnp.logical_not(is_me(owner_rows[k], owner_rep)))(
            functools.partial(left, "d4", k, d4s.at[0])
        )

    def along_z(o):
        zz = around(z, o)
        left("a2", zz, a2_like)
        left("d3", zz, a2_like)
        left("wz", zz, wz.at[z])

    def along_y(o):
        yy = around(y, o)
        left("d5", yy, gc.at[rep])
        left("c2", yy, c2s.at[yy])
        left("v2", yy, v2s.at[yy])
        left("c3", yy, oc.at[rep])
        left("wy", yy, wa.at[rep])

    def across(i):
        left("a3", i, a2_like)
        left("d2", i, a2_like)
        left("d6", i, gc.at[rep])
        left("c1", i, c1r.at[i])
        left("c4", i, oc.at[rep])
        left("wx", i, wa.at[rep])

    def cores(m):
        left("a4", m, a2_like)
        left("d1", m, a2_like)

    loop(1, n, along_z)
    loop(1, n, along_y)
    loop(0, n, across)
    loop(0, 2 * n, cores)
    for i in range(1, 4):
        left("wc", lax.rem(spot + i, 4), wc.at[spot])
    left("v1", 0, v1r)
    for out in outs:
        out.wait()


def settle_kernel(*refs):
    ins, outs, held = refs[:4], refs[4:8], refs[8:12]
    sem = refs[12]
    loads = [pltpu.make_async_copy(ins[i], held[i], sem.at[i]) for i in range(4)]
    stores = [pltpu.make_async_copy(held[i], outs[i], sem.at[4 + i]) for i in range(4)]
    for one in loads:
        one.start()
    for load, store in zip(loads, stores):
        load.wait()
        store.start()
    for one in stores:
        one.wait()


def settle(*arrays):
    anywhere = pl.BlockSpec(memory_space=pl.ANY)
    return pl.pallas_call(
        settle_kernel,
        out_shape=tuple(jax.ShapeDtypeStruct(a.shape, a.dtype) for a in arrays),
        in_specs=[anywhere] * 4,
        out_specs=(anywhere,) * 4,
        scratch_shapes=[pltpu.VMEM(a.shape, a.dtype) for a in arrays]
        + [pltpu.SemaphoreType.DMA((8,))],
        compiler_params=pltpu.CompilerParams(vmem_limit_bytes=VMEM_MIB * 1024 * 1024),
        name="settle",
    )(*arrays)


def on_device(feats, weight, weight_mask, tile_vals, edge_mask, tile_pos, grad_out):
    reps = lax.axis_size("rep")
    n = reps // 2
    block, width = feats.shape
    tiles, side, _ = tile_vals.shape
    rows = block // (4 * n)
    share = width // reps
    places, total = semaphore_places(n)
    chunked = (reps, 2 * rows, width)
    piece = (2, rows, width)
    slices = (share, width)

    def vm(shape, kind=BF):
        return pltpu.VMEM(shape, kind)

    scratch = [
        vm(piece), vm((block // side, side, width)), vm((width, width)), vm((width, width), jnp.int32),
        vm((tiles, side, side)), vm((tiles, side, side), F32),
        vm((width, width)), vm((4 * n,) + piece),
        vm((tiles, side, side)), vm((tiles, side, side)),
        vm((tiles, side, width)), vm((tiles, side, width)), vm((tiles, side, width)),
        vm((2 * side, tiles * side)), vm((4 * n,) + piece),
        vm((2 * n,) + piece), vm((n,) + piece), vm((n,) + piece), vm((n,) + piece), vm((n,) + piece),
        vm(piece, F32), vm(piece), vm((reps,) + piece),
        vm(chunked), vm((n,) + chunked[1:]), vm((n,) + chunked[1:]), vm((n,) + chunked[1:]),
        vm(chunked[1:], F32), vm(chunked),
        vm((2 * block // (2 * side), width, 2 * side)), vm((block // side, side, tiles * side)),
        vm((width, width), F32), vm((reps,) + slices), vm((n,) + slices), vm((n,) + slices), vm((n,) + slices),
        vm((n,) + slices, F32),
        vm((4, share, width), F32), vm((reps, share, width), F32), vm((width, width), F32),
        vm((tiles, side, side), F32), vm((block, width)),
        pltpu.SemaphoreType.DMA((total,)), pltpu.SemaphoreType.DMA((total,)),
        pltpu.SemaphoreType.DMA((6,)),
    ]
    anywhere = pl.BlockSpec(memory_space=pl.ANY)
    out, fgrad, wgrad, edge = pl.pallas_call(
        functools.partial(kernel, n, places),
        out_shape=(
            jax.ShapeDtypeStruct(chunked, BF),
            jax.ShapeDtypeStruct((block, width), BF),
            jax.ShapeDtypeStruct((width, width), F32),
            jax.ShapeDtypeStruct((tiles, side, side), F32),
        ),
        in_specs=[pl.BlockSpec(memory_space=pltpu.SMEM)] + [anywhere] * 6,
        out_specs=(anywhere,) * 4,
        scratch_shapes=scratch,
        compiler_params=pltpu.CompilerParams(
            collective_id=0, has_side_effects=True, vmem_limit_bytes=VMEM_MIB * 1024 * 1024
        ),
        cost_estimate=pl.CostEstimate(
            flops=3_000_000_000, bytes_accessed=5_000_000, transcendentals=0
        ),
        name="layer",
    )(
        tile_pos,
        feats.reshape((reps,) + piece),
        grad_out.reshape(block // side, side, width),
        weight,
        weight_mask,
        tile_vals,
        edge_mask,
    )
    return settle(out.reshape(block, width), fgrad, wgrad, edge)


def solution(mesh):
    placed = (
        P("row", None),
        P(),
        P(),
        P(("row", "rep"), None, None),
        P(("row", "rep"), None, None),
        P(("row", "rep")),
        P("row", None),
    )
    return jax.shard_map(
        on_device,
        mesh=mesh,
        in_specs=placed,
        out_specs=(P("row", None), P("row", None), P(), P(("row", "rep"), None, None)),
        check_vma=False,
    )
```

```python
import functools

import jax
import jax.numpy as jnp
from jax import lax
from jax.experimental import pallas as pl
from jax.experimental.pallas import tpu as pltpu
from jax.sharding import PartitionSpec as P

BF = jnp.bfloat16
F32 = jnp.float32
VMEM_MIB = 56


def semaphore_places(n):
    counts = dict(
        a1=2, a2=n, a3=n, a4=2 * n,
        d1=2 * n, d2=n, d3=n, d4=2, d5=n, d6=n,
        c1=n, c2=n, c3=n, c4=n,
        v1=1, v2=n, wz=n, wc=4, wy=n, wx=n,
    )
    places, total = {}, 0
    for name, count in counts.items():
        places[name] = total
        total += count
    return places, total


def loop(low, high, step):
    def run(i, carry):
        step(i)
        return carry

    lax.fori_loop(low, high, run, 0)


def kernel(
    n, places,
    pos_ref, feats_h, gout_h, w_h, wm_h, tv_h, em_h,
    out_h, fg_h, wg_h, ge_h,
    chunk, gout, w, wm, tv, em,
    weff, pj, mk, mkt, gs, rsf, rs, lhs, pb,
    d1r, d2s, d2r, d3s, d3r, d3o, d4s, gc,
    yb, c1r, c2s, c2r, c2o, oc,
    pbt, lf, wl, wv, v1r, v2s, v2r, wz, wc, wa, wgo, ge, fg,
    send, recv, local,
):
    row, rep = lax.axis_index("row"), lax.axis_index("rep")
    z, xl, c = row // 4, row // 2 % 2, row % 2
    xh, y = rep // n, rep % n
    reps = 2 * n
    tiles, side, _ = tv.shape
    width = w.shape[0]
    piece_rows = pj.shape[2]
    per_side = gout.shape[0]
    ppt = side // piece_rows
    block = per_side * side

    def row_of(zz, xx, cc):
        return zz * 4 + xx * 2 + cc

    core_row, lo_row, both_row = row_of(z, xl, 1 - c), row_of(z, 1 - xl, c), row_of(z, 1 - xl, 1 - c)
    hi_rep = (1 - xh) * n + y
    mine = (c * 2 + xl) * n + z

    def around(at, o):
        return lax.rem(at + o, n)

    def copy(name, i, j, src, dst, to_row, to_rep):
        return pltpu.make_async_remote_copy(
            src_ref=src,
            dst_ref=dst,
            send_sem=send.at[places[name] + i],
            recv_sem=recv.at[places[name] + j],
            device_id=(to_row, to_rep),
            device_id_type=pl.DeviceIdType.MESH,
        )

    def arrived(name, j, ref):
        copy(name, 0, j, ref, ref, core_row, rep).wait_recv()

    def left(name, i, ref):
        copy(name, i, 0, ref, ref, core_row, rep).wait_send()

    owner_rows, owner_rep = [k * reps + rep for k in range(2)], mine // 2
    own_half = lax.rem(mine, 2)
    section, group = row // reps, lax.rem(row, reps)
    part_rows, parts = [], []
    for e in range(2):
        p = 2 * rep + e
        parts.append(p)
        part_rows.append(row_of(lax.rem(p, n), lax.rem(p // n, 2), p // (2 * n)))

    def is_me(r, q):
        return jnp.logical_and(r == row, q == rep)

    ins = []
    for i, (src, dst) in enumerate(
        ((feats_h.at[rep], chunk), (tv_h, tv), (em_h, em), (gout_h, gout), (w_h, w), (wm_h, wm))
    ):
        ins.append(pltpu.make_async_copy(src, dst, local.at[i]))
        ins[-1].start()

    barrier = pltpu.get_barrier_semaphore()

    def greet(r, q):
        pl.semaphore_signal(barrier, inc=1, device_id=(r, q), device_id_type=pl.DeviceIdType.MESH)

    greet(core_row, rep)
    greet(lo_row, rep)
    greet(both_row, rep)
    greet(row, hi_rep)
    loop(1, n, lambda o: greet(row_of(around(z, o), xl, c), rep))
    loop(1, n, lambda o: greet(row, xh * n + around(y, o)))
    expected = 4 + 2 * (n - 1)
    for k in range(2):
        for r, q in ((owner_rows[k], owner_rep), (part_rows[k], group)):
            other = jnp.logical_not(is_me(r, q))
            pl.when(other)(functools.partial(greet, r, q))
            expected = expected + other.astype(jnp.int32)

    ins[0].wait()
    pl.semaphore_wait(barrier, expected)

    def scatter_piece(e):
        src, dst = chunk.at[e], pj.at[parts[e], section]
        same = is_me(part_rows[e], group)

        @pl.when(jnp.logical_not(same))
        def _():
            copy("a1", e, section, src, dst, part_rows[e], group).start()

        @pl.when(same)
        def _():
            pltpu.make_async_copy(src, dst, recv.at[places["a1"] + section]).start()

    scatter_piece(0)
    scatter_piece(1)

    picks = []
    for t in range(tiles):
        pos = pos_ref[t]
        slot = jnp.maximum(pos, 0)
        picks.append(
            (
                pos >= 0,
                lax.rem(slot // per_side, per_side),
                slot // (per_side * per_side),
                lax.rem(slot, per_side),
            )
        )

    ins[1].wait()
    ins[2].wait()
    ins[3].wait()
    for t in range(tiles):
        product = tv[t].astype(F32) * em[t]
        mk[t] = product.astype(BF)
        mkt[t] = product.T.astype(BF)
        gs[t] = gout[picks[t][1]]

    def chosen(cond, tile):
        return lax.select_n(cond, jnp.zeros_like(tile), tile)

    def backward_tile(jj):
        for k in range(2):
            for t in range(tiles):
                live, _, kt, jt = picks[t]
                cond = jnp.logical_and(live, jnp.logical_and(kt == k, jt == jj))
                lhs[k * side:(k + 1) * side, t * side:(t + 1) * side] = chosen(cond, mkt[t])
        total = jnp.dot(lhs[...], gs[...].reshape(tiles * side, width), preferred_element_type=F32)
        total = total.astype(BF)
        for k in range(2):
            pb[pl.ds(jj * ppt, ppt), k] = total[k * side:(k + 1) * side].reshape(ppt, piece_rows, width)

    quarter_tiles = n // ppt

    def send_quarter(x):
        def one(i):
            m = x * n + i
            copy("d1", m, m, pb.at[(1 - c) * 2 * n + m], d1r.at[m], core_row, rep).start()

        first = ((1 - c) * 2 + x) * quarter_tiles
        loop(0, quarter_tiles, lambda i: backward_tile(first + i))
        loop(0, n, one)

    send_quarter(1 - xl)
    send_quarter(xl)

    arrived("a1", 0, chunk.at[0])
    arrived("a1", 1, chunk.at[0])

    def pass_lo(zz):
        p = (c * 2 + xl) * n + zz
        copy("a3", zz, zz, pj.at[p], pj.at[p], lo_row, rep).start()

    def pass_core(m):
        p = c * 2 * n + m
        copy("a4", m, m, pj.at[p], pj.at[p], core_row, rep).start()

    def pass_z(o):
        zz = around(z, o)
        copy("a2", zz, z, pj.at[mine], pj.at[mine], row_of(zz, xl, c), rep).start()

    pass_lo(z)
    loop(1, n, pass_z)
    pass_core(xl * n + z)

    loop(0, 2 * quarter_tiles, lambda i: backward_tile(c * 2 * quarter_tiles + i))

    def d2_step(o):
        zz = around(z, o)
        m = (1 - xl) * n + zz
        arrived("d1", m, d1r.at[m])
        d2s[zz] = (pb[c * 2 * n + m].astype(F32) + d1r[m].astype(F32)).astype(BF)
        copy("d2", zz, zz, d2s.at[zz], d2r.at[zz], lo_row, rep).start()

    loop(1, n + 1, d2_step)

    chunk_rows = 2 * piece_rows
    deep = 2 * side // chunk_rows

    def turn(i):
        rows = pb[pl.ds(i * deep, deep)].reshape(2 * side, width)
        pbt[i] = rows.astype(F32).T.astype(BF)

    loop(0, 4 * n // deep, turn)

    def spread_row(i):
        for t in range(tiles):
            cond = jnp.logical_and(picks[t][0], picks[t][1] == i)
            lf[i, :, t * side:(t + 1) * side] = chosen(cond, mk[t])

    loop(0, per_side, spread_row)

    def a2_step(o):
        zz = around(z, o)
        arrived("a2", zz, a2_like)
        pass_lo(zz)
        pass_core(xl * n + zz)

    a2_like = pj.at[mine]
    loop(1, n, a2_step)

    def d3_sum(zz):
        m = xl * n + zz
        arrived("d1", m, d1r.at[m])
        arrived("d2", zz, d2r.at[zz])
        return pb[c * 2 * n + m].astype(F32) + d1r[m].astype(F32) + d2r[zz].astype(F32)

    def d3_step(o):
        zz = around(z, o)
        d3s[zz] = d3_sum(zz).astype(BF)
        copy("d3", zz, z, d3s.at[zz], d3r.at[z], row_of(zz, xl, c), rep).start()

    loop(1, n, d3_step)
    d3o[...] = d3_sum(z)

    def a3_step(o):
        zz = around(z, o)
        arrived("a3", zz, a2_like)
        pass_core((1 - xl) * n + zz)

    loop(0, n, a3_step)

    ins[4].wait()
    ins[5].wait()
    weff[...] = jnp.where(wm[...] != 0, w[...].astype(F32), 0.0).astype(BF)
    loop(0, 2 * n, lambda m: arrived("a4", m, a2_like))

    wl[...] = jnp.zeros_like(wl)

    def weight_step(i):
        rows = pj[pl.ds(i * deep, deep)].reshape(2 * side, width)
        wl[...] += jnp.dot(pbt[i], rows, preferred_element_type=F32)

    loop(0, 4 * n // deep, weight_step)
    wv[...] = wl[...].T.astype(BF).reshape(wv.shape)
    away = wv.at[pl.ds((1 - xh) * n, n)]
    copy("v1", 0, 0, away, v1r, row, hi_rep).start()

    for t in range(tiles):
        _, _, kt, jt = picks[t]
        rsf[t] = pj[pl.ds(jt * ppt, ppt), kt].reshape(side, width)
    rs[...] = (
        jnp.dot(rsf[...].reshape(tiles * side, width), weff[...], preferred_element_type=F32)
        .astype(BF)
        .reshape(tiles, side, width)
    )

    chunks_pair = 2 * side // (2 * piece_rows)
    pairs_half = block // 2 // (2 * side)

    def forward_pair(u):
        mine_rows = lf[pl.ds(2 * u, 2)].reshape(2 * side, tiles * side)
        total = jnp.dot(mine_rows, rs[...].reshape(tiles * side, width), preferred_element_type=F32)
        yb[pl.ds(u * chunks_pair, chunks_pair)] = total.astype(BF).reshape(
            chunks_pair, 2 * piece_rows, width
        )

    loop(0, pairs_half, lambda i: forward_pair((1 - xh) * pairs_half + i))

    def c1_step(o):
        yy = around(y, o)
        copy("c1", yy, yy, yb.at[(1 - xh) * n + yy], c1r.at[yy], row, hi_rep).start()

    loop(1, n + 1, c1_step)

    def d3_add(o):
        zz = around(z, o)
        arrived("d3", zz, d3r.at[zz])
        d3o[...] += d3r[zz].astype(F32)

    loop(1, n, d3_add)
    d4s[...] = d3o[...].astype(BF)
    for k in range(2):
        same = is_me(owner_rows[k], owner_rep)
        src, dst = d4s.at[k], gc.at[owner_rep, own_half]

        @pl.when(jnp.logical_not(same))
        def _(src=src, dst=dst, k=k):
            copy("d4", k, own_half, src, dst, owner_rows[k], owner_rep).start()

        @pl.when(same)
        def _(src=src, dst=dst):
            pltpu.make_async_copy(src, dst, recv.at[places["d4"] + own_half]).start()

    loop(0, pairs_half, lambda i: forward_pair(xh * pairs_half + i))

    def pass_hi(name, ref, yy):
        at = xh * n + yy
        copy(name, yy, yy, ref.at[at], ref.at[at], row, hi_rep).start()

    def pass_y(name, ref, o):
        yy = around(y, o)
        copy(name, yy, y, ref.at[rep], ref.at[rep], row, xh * n + yy).start()

    copy("v1", 0, 0, away, v1r, row, hi_rep).wait_recv()

    def v2_step(o):
        yy = around(y, o)
        v2s[yy] = (wv[xh * n + yy].astype(F32) + v1r[yy].astype(F32)).astype(BF)
        copy("v2", yy, y, v2s.at[yy], v2r.at[y], row, xh * n + yy).start()

    loop(1, n, v2_step)
    wz[z] = wv[rep].astype(F32) + v1r[y].astype(F32)

    def c2_sum(yy):
        arrived("c1", yy, c1r.at[yy])
        return yb[xh * n + yy].astype(F32) + c1r[yy].astype(F32)

    def c2_step(o):
        yy = around(y, o)
        c2s[yy] = c2_sum(yy).astype(BF)
        copy("c2", yy, y, c2s.at[yy], c2r.at[y], row, xh * n + yy).start()

    loop(1, n, c2_step)
    c2o[...] = c2_sum(y)

    def v2_add(o):
        yy = around(y, o)
        arrived("v2", yy, v2r.at[yy])
        wz[z] += v2r[yy].astype(F32)

    loop(1, n, v2_add)

    def wz_step(o):
        zz = around(z, o)
        copy("wz", zz, z, wz.at[z], wz.at[z], row_of(zz, xl, c), rep).start()

    loop(1, n, wz_step)

    arrived("d4", 0, d4s.at[0])
    arrived("d4", 1, d4s.at[0])
    pass_hi("d6", gc, y)
    loop(1, n, lambda o: pass_y("d5", gc, o))

    def relay(got, gone, ref, o):
        yy = around(y, o)
        arrived(got, yy, ref.at[rep])
        pass_hi(gone, ref, yy)


    def c2_add(o):
        yy = around(y, o)
        arrived("c2", yy, c2r.at[yy])
        c2o[...] += c2r[yy].astype(F32)

    loop(1, n, lambda o: arrived("wz", around(z, o), wz.at[z]))
    spot = xl * 2 + c
    wc[spot] = functools.reduce(jnp.add, [wz[i] for i in range(n)])
    for r, s in (
        (core_row, xl * 2 + 1 - c), (lo_row, (1 - xl) * 2 + c), (both_row, (1 - xl) * 2 + 1 - c)
    ):
        copy("wc", s, spot, wc.at[spot], wc.at[spot], r, rep).start()

    loop(1, n, c2_add)

    oc[rep] = c2o[...].astype(BF)
    pass_hi("c4", oc, y)
    loop(1, n, lambda o: pass_y("c3", oc, o))

    def edge_tile(t):
        scores = lax.dot_general(gs[t], rs[t], (((1,), (1,)), ((), ())), preferred_element_type=F32)
        ge[t] = chosen(picks[t][0], tv[t].astype(F32) * scores)

    for t in range(tiles // 2):
        edge_tile(t)

    loop(1, n, lambda o: relay("d5", "d6", gc, o))

    for t in range(tiles // 2, tiles):
        edge_tile(t)
    outs = [pltpu.make_async_copy(ge, ge_h, local.at[0])]
    outs[-1].start()

    for i in range(1, 4):
        arrived("wc", lax.rem(spot + i, 4), wc.at[spot])
    wa[rep] = (wc[0] + wc[1]) + (wc[2] + wc[3])
    pass_hi("wx", wa, y)
    loop(1, n, lambda o: pass_y("wy", wa, o))

    loop(1, n, lambda o: relay("c3", "c4", oc, o))

    loop(0, n, lambda yy: arrived("d6", yy, gc.at[rep]))
    fg[...] = lax.dot_general(
        gc[...].reshape(block, width), weff[...], (((1,), (1,)), ((), ())), preferred_element_type=F32
    ).astype(BF)
    outs.append(pltpu.make_async_copy(fg, fg_h, local.at[1]))
    outs[-1].start()

    loop(1, n, lambda o: relay("wy", "wx", wa, o))
    loop(0, n, lambda yy: arrived("c4", yy, oc.at[rep]))
    outs.append(pltpu.make_async_copy(oc, out_h, local.at[2]))
    outs[-1].start()
    loop(0, n, lambda yy: arrived("wx", yy, wa.at[rep]))
    wgo[...] = jnp.where(wm[...] != 0, wa[...].reshape(width, width), 0.0)
    outs.append(pltpu.make_async_copy(wgo, wg_h, local.at[3]))
    outs[-1].start()

    for k in range(2):
        pl.when(jnp.logical_not(is_me(part_rows[k], group)))(functools.partial(left, "a1", k, chunk.at[0]))
        pl.when(jnp.logical_not(is_me(owner_rows[k], owner_rep)))(
            functools.partial(left, "d4", k, d4s.at[0])
        )

    def along_z(o):
        zz = around(z, o)
        left("a2", zz, a2_like)
        left("d3", zz, a2_like)
        left("wz", zz, wz.at[z])

    def along_y(o):
        yy = around(y, o)
        left("d5", yy, gc.at[rep])
        left("c2", yy, c2s.at[yy])
        left("v2", yy, v2s.at[yy])
        left("c3", yy, oc.at[rep])
        left("wy", yy, wa.at[rep])

    def across(i):
        left("a3", i, a2_like)
        left("d2", i, a2_like)
        left("d6", i, gc.at[rep])
        left("c1", i, c1r.at[i])
        left("c4", i, oc.at[rep])
        left("wx", i, wa.at[rep])

    def cores(m):
        left("a4", m, a2_like)
        left("d1", m, a2_like)

    loop(1, n, along_z)
    loop(1, n, along_y)
    loop(0, n, across)
    loop(0, 2 * n, cores)
    for i in range(1, 4):
        left("wc", lax.rem(spot + i, 4), wc.at[spot])
    left("v1", 0, v1r)
    for out in outs:
        out.wait()


def settle_kernel(*refs):
    ins, outs, held = refs[:4], refs[4:8], refs[8:12]
    sem = refs[12]
    loads = [pltpu.make_async_copy(ins[i], held[i], sem.at[i]) for i in range(4)]
    stores = [pltpu.make_async_copy(held[i], outs[i], sem.at[4 + i]) for i in range(4)]
    for one in loads:
        one.start()
    for load, store in zip(loads, stores):
        load.wait()
        store.start()
    for one in stores:
        one.wait()


def settle(*arrays):
    anywhere = pl.BlockSpec(memory_space=pl.ANY)
    return pl.pallas_call(
        settle_kernel,
        out_shape=tuple(jax.ShapeDtypeStruct(a.shape, a.dtype) for a in arrays),
        in_specs=[anywhere] * 4,
        out_specs=(anywhere,) * 4,
        scratch_shapes=[pltpu.VMEM(a.shape, a.dtype) for a in arrays]
        + [pltpu.SemaphoreType.DMA((8,))],
        compiler_params=pltpu.CompilerParams(vmem_limit_bytes=VMEM_MIB * 1024 * 1024),
        name="settle",
    )(*arrays)


def on_device(feats, weight, weight_mask, tile_vals, edge_mask, tile_pos, grad_out):
    reps = lax.axis_size("rep")
    n = reps // 2
    block, width = feats.shape
    tiles, side, _ = tile_vals.shape
    rows = block // (4 * n)
    share = width // reps
    places, total = semaphore_places(n)
    chunked = (reps, 2 * rows, width)
    piece = (2, rows, width)
    slices = (share, width)

    def vm(shape, kind=BF):
        return pltpu.VMEM(shape, kind)

    scratch = [
        vm(piece), vm((block // side, side, width)), vm((width, width)), vm((width, width), jnp.int32),
        vm((tiles, side, side)), vm((tiles, side, side), F32),
        vm((width, width)), vm((4 * n,) + piece),
        vm((tiles, side, side)), vm((tiles, side, side)),
        vm((tiles, side, width)), vm((tiles, side, width)), vm((tiles, side, width)),
        vm((2 * side, tiles * side)), vm((4 * n,) + piece),
        vm((2 * n,) + piece), vm((n,) + piece), vm((n,) + piece), vm((n,) + piece), vm((n,) + piece),
        vm(piece, F32), vm(piece), vm((reps,) + piece),
        vm(chunked), vm((n,) + chunked[1:]), vm((n,) + chunked[1:]), vm((n,) + chunked[1:]),
        vm(chunked[1:], F32), vm(chunked),
        vm((2 * block // (2 * side), width, 2 * side)), vm((block // side, side, tiles * side)),
        vm((width, width), F32), vm((reps,) + slices), vm((n,) + slices), vm((n,) + slices), vm((n,) + slices),
        vm((n,) + slices, F32),
        vm((4, share, width), F32), vm((reps, share, width), F32), vm((width, width), F32),
        vm((tiles, side, side), F32), vm((block, width)),
        pltpu.SemaphoreType.DMA((total,)), pltpu.SemaphoreType.DMA((total,)),
        pltpu.SemaphoreType.DMA((6,)),
    ]
    anywhere = pl.BlockSpec(memory_space=pl.ANY)
    out, fgrad, wgrad, edge = pl.pallas_call(
        functools.partial(kernel, n, places),
        out_shape=(
            jax.ShapeDtypeStruct(chunked, BF),
            jax.ShapeDtypeStruct((block, width), BF),
            jax.ShapeDtypeStruct((width, width), F32),
            jax.ShapeDtypeStruct((tiles, side, side), F32),
        ),
        in_specs=[pl.BlockSpec(memory_space=pltpu.SMEM)] + [anywhere] * 6,
        out_specs=(anywhere,) * 4,
        scratch_shapes=scratch,
        compiler_params=pltpu.CompilerParams(
            collective_id=0, has_side_effects=True, vmem_limit_bytes=VMEM_MIB * 1024 * 1024
        ),
        cost_estimate=pl.CostEstimate(
            flops=3_000_000_000, bytes_accessed=5_000_000, transcendentals=0
        ),
        name="layer",
    )(
        tile_pos,
        feats.reshape((reps,) + piece),
        grad_out.reshape(block // side, side, width),
        weight,
        weight_mask,
        tile_vals,
        edge_mask,
    )
    return settle(out.reshape(block, width), fgrad, wgrad, edge)


def solution(mesh):
    placed = (
        P("row", None),
        P(),
        P(),
        P(("row", "rep"), None, None),
        P(("row", "rep"), None, None),
        P(("row", "rep")),
        P("row", None),
    )
    return jax.shard_map(
        on_device,
        mesh=mesh,
        in_specs=placed,
        out_specs=(P("row", None), P("row", None), P(), P(("row", "rep"), None, None)),
        check_vma=False,
    )
```
